32 devices in a mesh: cuts: 8 (over y, x, core), tile: 4 (over z).
Axes of the slice: x: 2, y: 2, z: 4, core: 2. Of those that a mesh axis runs over, the one named last changes fastest.
Arguments:
- probes: float32 [8, 8, 16, 4, 128], P('cuts', None, None, 'tile'), may hold values from -6 to 6
- test_block: float32 [8, 8, 16, 4, 128], P('cuts', None, None, 'tile'), may hold values from -6 to 6
- band_edge: float32 [8, 4, 128], P(None, 'tile'), may hold values from -3 to 3
- slice_hop: float32 [8], replicated, may hold values from 0.5 to 40
- cross_hop: float32 [2, 8, 8], replicated, may hold values from -0.4 to 0.4
- deform: float32 [6, 8, 8], replicated, may hold values from -0.4 to 0.4
- strain_elastic: float32 [8, 16, 6, 32], P('cuts', 'tile'), may hold values from -1 to 1
- strain_ids: int32 [16], replicated, may hold values from 0 to 15, as said below
Outputs:
- moment_fields: float32 [2, 2, 8, 8, 16, 4, 128], P(None, None, 'cuts', None, None, 'tile')
- projected: float32 [4, 2, 16, 16], replicated
The draws below stay inside these ranges and needn't reach their ends.
Inputs may be any that keep to these rules, and one draw needn't show every extreme that they name: strain_ids is a permutation; subtile g belongs to index g // 4 of tile, and slots i belong to index i // 4. The 4 slots of one index of tile hold at most 2 subtiles belonging to any one index, and exactly 2 for some index.
All inputs are finite; a program needn't handle non-finite values.
Results may differ from the reference program's by a relative error of at most 0.0085.
Values sent between devices are 32-bit elements; how exact they have to be, the bound alone decides.
A program may use at most 128 MiB of HBM per device.

```python
import math
import jax
import jax.numpy as jnp
import numpy as np
from jax import lax

BANDS = 8
PROBES = 16
PTS = 8
NMOM = 4
CX = 128
SUBC = 32
SLICES = 8
CYT = 4
NSUB = 4
NSUB_ALL = 16


def draw_strain_ids(key, part):
    sub_count = NSUB
    total = NSUB_ALL
    tile_count = total // sub_count
    key_shift, key_rank, key_order = jax.random.split(key, 3)
    shifts = jax.random.permutation(key_shift, tile_count)[:3]
    rank_keys = jax.random.split(key_rank, tile_count)
    position = jax.vmap(lambda single: jax.random.permutation(single, sub_count))(rank_keys)
    segment = jnp.where(position < sub_count // 2, 0, jnp.where(position < 3 * sub_count // 4, 1, 2))
    owners = (jnp.arange(tile_count)[:, None] - shifts[segment]) % tile_count
    shuffle = jax.random.permutation(key_order, total).reshape(tile_count, sub_count)
    ordering = owners * total + shuffle
    return jnp.argsort(ordering.reshape(-1)).astype(jnp.int32)


def levels(stream_key, extent, shards, low, largest):
    level = 1.0
    for dim, blocks in shards:
        draws = jax.random.uniform(jax.random.fold_in(jax.random.fold_in(stream_key, 6), dim), (blocks,), jnp.float32, low / len(shards), largest / len(shards))
        level = level * jnp.repeat(jnp.exp(draws), extent[dim] // blocks).reshape((-1,) + (1,) * (len(extent) - 1 - dim))
    return level


def gaussian(own_key, extent, width, reach, pieces=(), kind=jnp.bfloat16):
    entries = width * jax.random.normal(own_key, extent, jnp.float32)
    if pieces:
        entries = entries * levels(own_key, extent, pieces, -0.22, 0.18)
    return jnp.clip(entries, -reach, reach).astype(kind)


def setup_inputs(seed: int = 0) -> dict:
    streams_of = jax.random.split(jax.random.key(seed), 9)
    probes = gaussian(streams_of[0], (SLICES, BANDS, PROBES, CYT, CX), 1.0, 6.0, ((0, 8), (3, 4)), jnp.float32)
    test_block = gaussian(streams_of[1], (SLICES, BANDS, PROBES, CYT, CX), 1.0, 6.0, ((0, 8), (3, 4)), jnp.float32)
    band_edge = jnp.clip(jax.random.uniform(streams_of[2], (BANDS, CYT, CX), jnp.float32, -3.0, 3.0) * levels(streams_of[2], (BANDS, CYT, CX), ((1, 4),), -0.4, 0.0), -3.0, 3.0)
    slice_hop = jnp.clip(jnp.exp(jax.random.uniform(streams_of[3], (BANDS,), jnp.float32, math.log(0.5), math.log(40.0))), 0.5, 40.0)
    cross_hop = gaussian(streams_of[4], (2, BANDS, BANDS), 0.08, 0.4, (), jnp.float32)
    deform = gaussian(streams_of[5], (6, BANDS, BANDS), 0.08, 0.4, (), jnp.float32)
    strain_elastic = jnp.clip(jax.random.uniform(streams_of[6], (SLICES, NSUB_ALL, 6, SUBC), jnp.float32, -1.0, 1.0) * levels(streams_of[6], (SLICES, NSUB_ALL, 6, SUBC), ((0, 8), (1, 4)), -0.4, 0.0), -1.0, 1.0)
    strain_ids = draw_strain_ids(jax.random.fold_in(streams_of[8], 71), 0)
    return dict(probes=probes, test_block=test_block, band_edge=band_edge, slice_hop=slice_hop, cross_hop=cross_hop, deform=deform, strain_elastic=strain_elastic, strain_ids=strain_ids)


HIGHEST = lax.Precision.HIGHEST

def complex_times(former, latter):
    return jnp.stack([former[0] * latter[0] - former[1] * latter[1], former[0] * latter[1] + former[1] * latter[0]])

def complex_inverse(number):
    square = number[0] * number[0] + number[1] * number[1]
    return jnp.stack([number[0] / square, -number[1] / square])

def complex_power(base_value, exponent, bit_count):
    result = jnp.stack([jnp.ones_like(base_value[0]), jnp.zeros_like(base_value[0])])
    squared = base_value
    for bit_index in range(bit_count):
        bit_set = exponent // 2 ** bit_index % 2
        result = jnp.where(bit_set == 1, complex_times(result, squared), result)
        squared = complex_times(squared, squared)
    return result

def line_ratio(band_edge, slice_hop, real_part, imag_part):
    hopping = slice_hop[:, None, None]
    ratio_re = (real_part - band_edge) / hopping
    ratio_im = (imag_part + 0.0 * band_edge) / hopping
    disc_re = ratio_re * ratio_re - ratio_im * ratio_im - 4.0
    disc_im = 2.0 * ratio_re * ratio_im
    modulus = jnp.sqrt(disc_re * disc_re + disc_im * disc_im)
    root_re = jnp.sqrt(jnp.maximum(0.5 * (modulus + disc_re), 0.0))
    root_im = jnp.sqrt(jnp.maximum(0.5 * (modulus - disc_re), 0.0)) * jnp.where(disc_im >= 0.0, 1.0, -1.0)
    lower_re = 0.5 * (ratio_re - root_re)
    lower_im = 0.5 * (ratio_im - root_im)
    upper_re = 0.5 * (ratio_re + root_re)
    upper_im = 0.5 * (ratio_im + root_im)
    choose_low = lower_re * lower_re + lower_im * lower_im <= upper_re * upper_re + upper_im * upper_im
    alpha_re = jnp.where(choose_low, lower_re, upper_re)
    alpha_im = jnp.where(choose_low, lower_im, upper_im)
    return jnp.stack([-alpha_re, -alpha_im])

def line_kernel(decay_rate, slice_hop, length):
    bit_count = length.bit_length()
    exponents = jnp.arange(length + 1).reshape(-1, 1, 1, 1)
    powers = complex_power(decay_rate[:, None], exponents, bit_count)
    series = powers[:, :length] + powers[:, length:0:-1]
    unit_value = jnp.stack([jnp.ones_like(decay_rate[0]), jnp.zeros_like(decay_rate[0])])
    denominator = complex_times(unit_value - complex_times(decay_rate, decay_rate), unit_value - powers[:, length])
    leading = complex_times(-decay_rate / slice_hop[None, :, None, None], complex_inverse(denominator))
    profile = complex_times(leading[:, None], series)
    offsets = (np.arange(length)[:, None] - np.arange(length)[None, :]) % length
    return jnp.take(profile, jnp.asarray(offsets, dtype=jnp.int32), axis=1)

def apply_lines(kernel, amplitude):

    def contract(former, latter):
        return jnp.einsum('smbyx,mbpyx->sbpyx', former, latter, precision=HIGHEST)
    return jnp.stack([contract(kernel[0], amplitude[0]) - contract(kernel[1], amplitude[1]), contract(kernel[0], amplitude[1]) + contract(kernel[1], amplitude[0])])

def couple_cells(amplitude, cross_hop, strain_mix):
    widths = [(0, 0)] * 5
    toward_right = jnp.pad(amplitude[..., 1:], widths + [(0, 1)])
    toward_left = jnp.pad(amplitude[..., :-1], widths + [(1, 0)])
    upward = jnp.pad(amplitude[..., 1:, :], widths[:4] + [(0, 1), (0, 0)])
    downward = jnp.pad(amplitude[..., :-1, :], widths[:4] + [(1, 0), (0, 0)])
    hoppers = jnp.stack([cross_hop[0], cross_hop[0].T, cross_hop[1], cross_hop[1].T])
    nearby = jnp.stack([toward_right, toward_left, upward, downward])
    summed = jnp.einsum('dbc,dkscpyx->ksbpyx', hoppers, nearby, precision=HIGHEST)
    return summed + jnp.einsum('sbcyx,kscpyx->ksbpyx', strain_mix, amplitude, precision=HIGHEST)

def reference(probes, test_block, band_edge, slice_hop, cross_hop, deform, strain_elastic, strain_ids):
    slices = probes.shape[0]
    bands = probes.shape[1]
    rows_all = probes.shape[3]
    cols_all = probes.shape[4]
    placed = jnp.zeros_like(strain_elastic).at[:, strain_ids].set(strain_elastic)
    strain = jnp.transpose(placed, (0, 2, 1, 3)).reshape(slices, 6, rows_all, cols_all)
    symmetric = 0.5 * (deform + jnp.transpose(deform, (0, 2, 1)))
    strain_mix = jnp.einsum('skyx,kbc->sbcyx', strain, symmetric, precision=HIGHEST)
    source = jnp.stack([probes, jnp.zeros_like(probes)])
    moments = jnp.zeros((NMOM, 2) + probes.shape, jnp.float32)
    for point in range(PTS):
        angle = math.pi * (2 * point + 1) / PTS
        decay_rate = line_ratio(band_edge, slice_hop, math.cos(angle), math.sin(angle))
        kernel = line_kernel(decay_rate, slice_hop, slices)
        first_step = apply_lines(kernel, source)
        second_step = first_step + apply_lines(kernel, couple_cells(first_step, cross_hop, strain_mix))
        for order in range(NMOM):
            weight_re = math.cos((order + 1) * angle) / PTS
            weight_im = math.sin((order + 1) * angle) / PTS
            update = jnp.stack([weight_re * second_step[0] - weight_im * second_step[1], weight_re * second_step[1] + weight_im * second_step[0]])
            moments = moments.at[order].add(update)
    scale = (slices * bands * rows_all * cols_all) ** (-0.5)
    projected = jnp.einsum('sbqyx,nksbryx->nkqr', test_block, moments, precision=HIGHEST) * scale
    return (moments[:2], projected)
```

```python
import functools
import math

import jax
import jax.numpy as jnp
import numpy as np
from jax import lax
from jax.experimental import pallas as pl
from jax.experimental.pallas import tpu as pltpu
from jax.sharding import PartitionSpec as P

PTS = 8
HALF = PTS // 2
NMOM = 4
NFIELD = 2
MESH = pl.DeviceIdType.MESH

ANGLES = [math.pi * (2 * point + 1) / PTS for point in range(HALF)]


def line_green(edge, hop, length):
    half = length // 2
    parts = []
    for angle in ANGLES:
        zr, zi = math.cos(angle), math.sin(angle)
        modes = []
        for k in range(half + 1):
            shifted = (zr - edge) + (2.0 * math.cos(2 * math.pi * k / length)) * hop
            inverse = 1.0 / (shifted * shifted + zi * zi)
            modes.append((shifted * inverse, (-zi) * inverse))
        for comp in range(2):
            rows = []
            for d in range(half + 1):
                total = None
                for k in range(half + 1):
                    weight = (1.0 if k in (0, half) else 2.0) / length
                    term = modes[k][comp] * (weight * math.cos(2 * math.pi * k * d / length))
                    total = term if total is None else total + term
                rows.append(total)
            parts.append(rows)
    return parts


def kernel(
    dims,
    ids_ref,
    hop_ref,
    cross_ref,
    deform_ref,
    probe_ref,
    test_ref,
    edge_ref,
    elastic_ref,
    field_ref,
    proj_ref,
    slots,
    send,
    got,
    edges,
    green,
    mixer,
    first,
    second,
    back,
    home,
    final,
    part,
    part_tile,
    part_cut,
    send_sem,
    got_sem,
    edge_send,
    edge_sem,
    back_send,
    home_sem,
    tile_send,
    tile_sem,
    cut_send,
    cut_sem,
):
    S, T, B, R, X, NS, SC = dims
    W = min(S, R)
    npr = R // W
    half = S // 2
    D = half + 1
    F = 2 * HALF
    chunk = npr * B
    msg = chunk + 8
    ret = NMOM * chunk
    N = S * T
    cut = lax.axis_index("cuts")
    tile = lax.axis_index("tile")
    me = cut * T + tile

    barrier = pltpu.get_barrier_semaphore()

    def greet(off, carry):
        other = lax.rem(me + off, N)
        pl.semaphore_signal(
            barrier, inc=1, device_id=(other // T, lax.rem(other, T)), device_id_type=MESH
        )
        return carry

    lax.fori_loop(1, N, greet, 0)

    slots[...] = jnp.zeros_like(slots)
    for i in range(NS):
        slots[0:6, i * SC : (i + 1) * SC] = elastic_ref[i]
    held = slots[...]
    turned = [held] + [pltpu.roll(held, SC * d, 1) for d in range(1, NS)]
    lane = lax.broadcasted_iota(jnp.int32, (8, X), 1)
    group = lane // SC
    own_ids = [ids_ref[tile * NS + i] for i in range(NS)]
    for t in range(T):
        placed = jnp.zeros((8, X), jnp.float32)
        for i in range(NS):
            for g in range(NS):
                wanted = jnp.where(group == g, t * NS + g, -1)
                placed = jnp.where(wanted == own_ids[i], turned[(g - i) % NS], placed)
        for w in range(W):
            row = (t * W + w) * msg
            for i in range(npr):
                send[row + i * B : row + (i + 1) * B, :] = probe_ref[
                    pl.ds(w * npr + i, B, stride=R), :
                ]
            send[row + chunk : row + msg, :] = placed
    edges[1] = edge_ref[...]

    pl.semaphore_wait(barrier, N - 1)

    def message(target_tile, target_cut, off, near):
        source = (target_tile * W + lax.rem(target_cut, W)) * msg
        landing = (tile * S + cut) * msg
        skip = 0 if near else chunk
        return pltpu.make_async_remote_copy(
            src_ref=send.at[pl.ds(pl.multiple_of(source + skip, 8), msg - skip), :],
            dst_ref=got.at[pl.ds(pl.multiple_of(landing + skip, 8), msg - skip), :],
            send_sem=send_sem.at[off],
            recv_sem=got_sem.at[tile, cut],
            device_id=(target_cut, target_tile),
            device_id_type=MESH,
        )

    def edge_copy(side):
        return pltpu.make_async_remote_copy(
            src_ref=edge_ref,
            dst_ref=edges.at[2 - side],
            send_sem=edge_send.at[side],
            recv_sem=edge_sem.at[2 - side],
            device_id=(cut, tile + side - 1),
            device_id_type=MESH,
        )

    has_side = {0: tile > 0, 2: tile < T - 1}
    for side in (0, 2):
        pl.when(has_side[side])(lambda side=side: edge_copy(side).start())

    def each_other(act):
        def body(off, carry):
            other = lax.rem(me + off, N)
            there_cut, there_tile = other // T, lax.rem(other, T)
            near = jnp.abs(there_tile - tile) <= 1

            @pl.when(near)
            def _():
                act(there_tile, there_cut, off, True)

            @pl.when(jnp.logical_not(near))
            def _():
                act(there_tile, there_cut, off, False)

            return carry

        lax.fori_loop(1, N, body, 0)

    each_other(lambda t, c, off, near: message(t, c, off, near).start())
    here = pl.multiple_of((tile * S + cut) * msg, 8)
    mine = pl.multiple_of((tile * W + lax.rem(cut, W)) * msg, 8)
    got[pl.ds(here, msg), :] = send[pl.ds(mine, msg), :]

    band = lax.broadcasted_iota(jnp.int32, (B, X), 0)
    hop = jnp.zeros((B, X), jnp.float32)
    for b in range(B):
        hop = jnp.where(band == b, hop_ref[b], hop)

    def fill_green(row):
        parts = line_green(edges[row], hop, S)
        for f in range(F):
            for d in range(D):
                green[row, f * D + d] = parts[f][d]
        return parts

    parts = fill_green(1)
    for p in range(NMOM):
        for j in range(HALF):
            wr = 2.0 * math.cos((p + 1) * ANGLES[j]) / PTS
            wi = 2.0 * math.sin((p + 1) * ANGLES[j]) / PTS
            for d in range(D):
                re, im = parts[2 * j][d], parts[2 * j + 1][d]
                final[(p * D + d) * F + 2 * j] = wr * re - wi * im
                final[(p * D + d) * F + 2 * j + 1] = -(wr * im + wi * re)
    for side in (0, 2):

        @pl.when(has_side[side])
        def _(side=side):
            edge_copy(2 - side).wait_recv()
            fill_green(side)

    def arrived(t, c, off, near):
        skip = 0 if near else chunk
        place = got.at[pl.ds(pl.multiple_of((t * S + c) * msg + skip, 8), msg - skip), :]
        pltpu.make_async_remote_copy(
            src_ref=place,
            dst_ref=place,
            send_sem=send_sem.at[off],
            recv_sem=got_sem.at[t, c],
            device_id=(c, t),
            device_id_type=MESH,
        ).wait_recv()

    each_other(arrived)

    def solve_row(row):
        base = (tile + row - 1) * (S * msg)

        def body(b, carry):
            for i in range(npr):
                line = got[pl.ds(base + i * B + b, S, stride=msg), :]
                sums = [line]
                for d in range(1, half):
                    sums.append(pltpu.roll(line, d, 0) + pltpu.roll(line, S - d, 0))
                sums.append(pltpu.roll(line, half, 0))
                for f in range(F):
                    total = None
                    for d in range(D):
                        term = green[row, f * D + d, pl.ds(b, 1), :] * sums[d]
                        total = term if total is None else total + term
                    first[row, b, f * npr + i] = total
            return carry

        lax.fori_loop(0, B, body, 0)

    solve_row(1)
    for side in (0, 2):
        pl.when(has_side[side])(lambda side=side: solve_row(side))

        @pl.when(jnp.logical_not(has_side[side]))
        def _(side=side):
            def clear(b, carry):
                first[side, b] = jnp.zeros_like(first[side, 0])
                return carry

            lax.fori_loop(0, B, clear, 0)

    strain = []
    for k in range(6):
        total = None
        for t in range(T):
            term = got[pl.ds(t * S * msg + chunk + k, S, stride=msg), :]
            total = term if total is None else total + term
        strain.append(total)
    for b in range(B):
        for c in range(b, B):
            total = None
            for k in range(6):
                term = (0.5 * (deform_ref[k, b, c] + deform_ref[k, c, b])) * strain[k]
                total = term if total is None else total + term
            mixer[b, c] = total
            if c != b:
                mixer[c, b] = total

    lanes = lax.broadcasted_iota(jnp.int32, (1, 1, X), 2)
    block = max(1, 8 * 8 // S)
    pieces = F * npr // block

    def couple(step, carry):
        b, piece = step // pieces, lax.rem(step, pieces)
        pick = pl.ds(piece * block, block)
        right = left = stay = None
        for c in range(B):
            u = first[1, c, pick]
            up, down = first[2, c, pick], first[0, c, pick]
            a = cross_ref[0, b, c] * u
            l = cross_ref[0, c, b] * u
            s = mixer[b, c][None] * u + cross_ref[1, b, c] * up + cross_ref[1, c, b] * down
            right = a if right is None else right + a
            left = l if left is None else left + l
            stay = s if stay is None else stay + s
        flat = (block * S, X)
        right = pltpu.roll(right.reshape(flat), X - 1, 1).reshape(block, S, X)
        left = pltpu.roll(left.reshape(flat), 1, 1).reshape(block, S, X)
        stay = stay + jnp.where(lanes < X - 1, right, 0.0) + jnp.where(lanes > 0, left, 0.0)
        second[b, pick] = stay
        return carry

    lax.fori_loop(0, B * pieces, couple, 0)

    def moments(b, carry):
        for i in range(npr):
            ys = [second[b, f * npr + i] for f in range(F)]
            xs = [first[1, b, f * npr + i] for f in range(F)]
            for p in range(NMOM):
                total = None
                for j in range(HALF):
                    wr = 2.0 * math.cos((p + 1) * ANGLES[j]) / PTS
                    wi = 2.0 * math.sin((p + 1) * ANGLES[j]) / PTS
                    term = wr * xs[2 * j] - wi * xs[2 * j + 1]
                    total = term if total is None else total + term
                for d in range(D):
                    z = None
                    for f in range(F):
                        term = final[(p * D + d) * F + f, pl.ds(b, 1), :] * ys[f]
                        z = term if z is None else z + term
                    if d == 0:
                        total = total + z
                    elif d == half:
                        total = total + pltpu.roll(z, half, 0)
                    else:
                        total = total + pltpu.roll(z, d, 0) + pltpu.roll(z, S - d, 0)
                back[pl.ds((p * npr + i) * B + b, S, stride=ret), :] = total
        return carry

    lax.fori_loop(0, B, moments, 0)

    mates = (cut // W) * W
    rank = lax.rem(cut, W)

    def home_copy(off, inbound):
        other = lax.rem(rank + off, W)
        source = pl.multiple_of((mates + other) * ret, 8)
        landing = pl.multiple_of((other if inbound else rank) * ret, 8)
        return pltpu.make_async_remote_copy(
            src_ref=back.at[pl.ds(source, ret), :],
            dst_ref=home.at[pl.ds(landing, ret), :],
            send_sem=back_send.at[off],
            recv_sem=home_sem.at[other if inbound else rank],
            device_id=(mates + other, tile),
            device_id_type=MESH,
        )

    def run(low, high, act):
        def body(off, carry):
            act(off)
            return carry

        lax.fori_loop(low, high, body, 0)

    run(1, W, lambda off: home_copy(off, False).start())
    home[pl.ds(pl.multiple_of(rank * ret, 8), ret), :] = back[
        pl.ds(pl.multiple_of(cut * ret, 8), ret), :
    ]
    run(1, W, lambda off: home_copy(off, True).wait_recv())

    acc = None
    for b in range(B):
        rows = home[pl.ds(b, W * NMOM * npr, stride=B), :]
        term = lax.dot_general(
            test_ref[b * R : (b + 1) * R, :],
            rows,
            (((1,), (1,)), ((), ())),
            precision=lax.Precision.HIGHEST,
            preferred_element_type=jnp.float32,
        )
        acc = term if acc is None else acc + term
    scale = (S * B * T * X) ** (-0.5)
    part_tile[tile] = jnp.zeros_like(part)
    part_tile[tile, :, : NMOM * R] = acc * scale

    def tile_copy(off, inbound):
        other = lax.rem(tile + off, T)
        return pltpu.make_async_remote_copy(
            src_ref=part_tile.at[tile],
            dst_ref=part_tile.at[other if inbound else tile],
            send_sem=tile_send.at[off],
            recv_sem=tile_sem.at[other if inbound else tile],
            device_id=(cut, other),
            device_id_type=MESH,
        )

    def cut_copy(off, inbound):
        other = lax.rem(cut + off, S)
        return pltpu.make_async_remote_copy(
            src_ref=part_cut.at[cut],
            dst_ref=part_cut.at[other if inbound else cut],
            send_sem=cut_send.at[off],
            recv_sem=cut_sem.at[other if inbound else cut],
            device_id=(other, tile),
            device_id_type=MESH,
        )

    run(1, T, lambda off: tile_copy(off, False).start())
    for w in range(W):
        for p in range(NFIELD):
            for i in range(npr):
                row = w * ret + (p * npr + i) * B
                field_ref[pl.ds(p * B * R + w * npr + i, B, stride=R), :] = home[row : row + B, :]
    run(1, T, lambda off: tile_copy(off, True).wait_recv())
    total = part_tile[0]
    for t in range(1, T):
        total = total + part_tile[t]
    part_cut[cut] = total
    run(1, S, lambda off: cut_copy(off, False).start())

    each_other(lambda t, c, off, near: message(t, c, off, near).wait_send())
    for side in (0, 2):
        pl.when(has_side[side])(lambda side=side: edge_copy(side).wait_send())
    run(1, W, lambda off: home_copy(off, False).wait_send())
    run(1, T, lambda off: tile_copy(off, False).wait_send())
    run(1, S, lambda off: cut_copy(off, True).wait_recv())
    total = part_cut[0]
    for c in range(1, S):
        total = total + part_cut[c]
    proj_ref[...] = total
    run(1, S, lambda off: cut_copy(off, False).wait_send())


def on_device(
    S, T, probes, test_block, band_edge, slice_hop, cross_hop, deform, strain_elastic, strain_ids
):
    _, B, R, _, X = probes.shape
    NS, SC = strain_elastic.shape[1], strain_elastic.shape[3]
    dims = (S, T, B, R, X, NS, SC)
    W = min(S, R)
    npr = R // W
    D = S // 2 + 1
    F = 2 * HALF
    chunk = npr * B
    msg = chunk + 8
    ret = NMOM * chunk
    smem = pl.BlockSpec(memory_space=pltpu.SMEM)
    vmem = pl.BlockSpec(memory_space=pltpu.VMEM)
    f32 = jnp.float32
    dma = pltpu.SemaphoreType.DMA
    fields, proj = pl.pallas_call(
        functools.partial(kernel, dims),
        out_shape=(
            jax.ShapeDtypeStruct((NFIELD * B * R, X), f32),
            jax.ShapeDtypeStruct((R, X), f32),
        ),
        in_specs=[smem] * 4 + [vmem] * 4,
        out_specs=(vmem, vmem),
        scratch_shapes=[
            pltpu.VMEM((8, X), f32),
            pltpu.VMEM((T * W * msg, X), f32),
            pltpu.VMEM((T * S * msg, X), f32),
            pltpu.VMEM((3, B, X), f32),
            pltpu.VMEM((3, F * D, B, X), f32),
            pltpu.VMEM((B, B, S, X), f32),
            pltpu.VMEM((3, B, F * npr, S, X), f32),
            pltpu.VMEM((B, F * npr, S, X), f32),
            pltpu.VMEM((S * ret, X), f32),
            pltpu.VMEM((W * ret, X), f32),
            pltpu.VMEM((NMOM * D * F, B, X), f32),
            pltpu.VMEM((R, X), f32),
            pltpu.VMEM((T, R, X), f32),
            pltpu.VMEM((S, R, X), f32),
            dma((S * T,)),
            dma((T, S)),
            dma((3,)),
            dma((3,)),
            dma((W,)),
            dma((W,)),
            dma((T,)),
            dma((T,)),
            dma((S,)),
            dma((S,)),
        ],
        compiler_params=pltpu.CompilerParams(
            collective_id=0, has_side_effects=True, vmem_limit_bytes=48 * 1024 * 1024
        ),
    )(
        strain_ids,
        slice_hop,
        cross_hop,
        deform,
        probes.reshape(B * R, X),
        test_block.reshape(B * R, X),
        band_edge.reshape(B, X),
        strain_elastic[0],
    )
    fields = fields.reshape(NFIELD, 1, 1, B, R, 1, X)
    fields = jnp.concatenate([fields, jnp.zeros_like(fields)], axis=1)
    proj = proj[:, : NMOM * R].reshape(R, W, NMOM, npr)
    proj = jnp.transpose(proj, (2, 0, 1, 3)).reshape(NMOM, 1, R, R)
    return fields, jnp.concatenate([proj, jnp.zeros_like(proj)], axis=1)


def solution(mesh):
    placed = (
        P("cuts", None, None, "tile", None),
        P("cuts", None, None, "tile", None),
        P(None, "tile", None),
        P(),
        P(),
        P(),
        P("cuts", "tile", None, None),
        P(),
    )
    return jax.shard_map(
        functools.partial(on_device, mesh.shape["cuts"], mesh.shape["tile"]),
        mesh=mesh,
        in_specs=placed,
        out_specs=(P(None, None, "cuts", None, None, "tile", None), P()),
        check_vma=False,
    )
```

```python
import functools
import math

import jax
import jax.numpy as jnp
import numpy as np
from jax import lax
from jax.experimental import pallas as pl
from jax.experimental.pallas import tpu as pltpu
from jax.sharding import PartitionSpec as P

PTS = 8
HALF = PTS // 2
NMOM = 4
NFIELD = 2
MESH = pl.DeviceIdType.MESH

ANGLES = [math.pi * (2 * point + 1) / PTS for point in range(HALF)]


def line_green(edge, hop, length):
    half = length // 2
    parts = []
    for angle in ANGLES:
        zr, zi = math.cos(angle), math.sin(angle)
        modes = []
        for k in range(half + 1):
            shifted = (zr - edge) + (2.0 * math.cos(2 * math.pi * k / length)) * hop
            inverse = 1.0 / (shifted * shifted + zi * zi)
            modes.append((shifted * inverse, (-zi) * inverse))
        for comp in range(2):
            rows = []
            for d in range(half + 1):
                total = None
                for k in range(half + 1):
                    weight = (1.0 if k in (0, half) else 2.0) / length
                    term = modes[k][comp] * (weight * math.cos(2 * math.pi * k * d / length))
                    total = term if total is None else total + term
                rows.append(total)
            parts.append(rows)
    return parts


def kernel(
    dims,
    ids_in,
    hop_in,
    cross_in,
    deform_in,
    probe_in,
    test_in,
    edge_in,
    elastic_in,
    field_ref,
    proj_ref,
    ids_ref,
    hop_ref,
    cross_ref,
    deform_ref,
    probe_ref,
    elastic_ref,
    tests,
    slots,
    send,
    got,
    edges,
    green,
    mixer,
    first,
    second,
    back,
    home,
    final,
    parts_all,
    load_sem,
    send_sem,
    got_sem,
    edge_send,
    edge_sem,
    back_send,
    home_sem,
    test_send,
    test_sem,
    part_send,
    part_sem,
):
    S, T, B, R, X, NS, SC = dims
    W = min(S, R)
    npr = R // W
    half = S // 2
    D = half + 1
    F = 2 * HALF
    chunk = npr * B
    msg = chunk + 8
    ret = NMOM * chunk
    kept = NFIELD * chunk
    N = S * T
    cut = lax.axis_index("cuts")
    tile = lax.axis_index("tile")
    me = cut * T + tile

    own_tests = pl.ds(pl.multiple_of(cut * (B * R), 8), B * R)
    loads = [
        pltpu.make_async_copy(src, dst, load_sem.at[n])
        for n, (src, dst) in enumerate(
            (
                (probe_in, probe_ref),
                (elastic_in, elastic_ref),
                (ids_in, ids_ref),
                (edge_in, edges.at[1]),
                (hop_in, hop_ref),
                (cross_in, cross_ref),
                (deform_in, deform_ref),
                (test_in, tests.at[own_tests, :]),
            )
        )
    ]
    for load in loads:
        load.start()
    barrier = pltpu.get_barrier_semaphore()

    def greet(off, carry):
        other = lax.rem(me + off, N)
        pl.semaphore_signal(
            barrier, inc=1, device_id=(other // T, lax.rem(other, T)), device_id_type=MESH
        )
        return carry

    lax.fori_loop(1, N, greet, 0)

    slots[...] = jnp.zeros_like(slots)
    for load in loads[:3]:
        load.wait()
    for k in range(6):
        for i in range(NS):
            slots[k : k + 1, i * SC : (i + 1) * SC] = elastic_ref[k, i : i + 1, :]
    held = slots[...]
    turned = [held] + [pltpu.roll(held, SC * d, 1) for d in range(1, NS)]
    lane = lax.broadcasted_iota(jnp.int32, (8, X), 1)
    group = lane // SC
    own_ids = [ids_ref[tile * NS + i] for i in range(NS)]
    for t in range(T):
        placed = jnp.zeros((8, X), jnp.float32)
        for i in range(NS):
            for g in range(NS):
                wanted = jnp.where(group == g, t * NS + g, -1)
                placed = jnp.where(wanted == own_ids[i], turned[(g - i) % NS], placed)
        for w in range(W):
            row = (t * W + w) * msg
            for i in range(npr):
                send[row + i * B : row + (i + 1) * B, :] = probe_ref[
                    pl.ds(w * npr + i, B, stride=R), :
                ]
            send[row + chunk : row + msg, :] = placed
    for load in loads[3:]:
        load.wait()

    pl.semaphore_wait(barrier, N - 1)

    def message(target_tile, target_cut, off, near):
        source = (target_tile * W + lax.rem(target_cut, W)) * msg
        landing = (tile * S + cut) * msg
        skip = 0 if near else chunk
        return pltpu.make_async_remote_copy(
            src_ref=send.at[pl.ds(pl.multiple_of(source + skip, 8), msg - skip), :],
            dst_ref=got.at[pl.ds(pl.multiple_of(landing + skip, 8), msg - skip), :],
            send_sem=send_sem.at[off],
            recv_sem=got_sem.at[tile, cut],
            device_id=(target_cut, target_tile),
            device_id_type=MESH,
        )

    def edge_copy(side):
        return pltpu.make_async_remote_copy(
            src_ref=edges.at[1],
            dst_ref=edges.at[2 - side],
            send_sem=edge_send.at[side],
            recv_sem=edge_sem.at[2 - side],
            device_id=(cut, tile + side - 1),
            device_id_type=MESH,
        )

    has_side = {0: tile > 0, 2: tile < T - 1}
    for side in (0, 2):
        pl.when(has_side[side])(lambda side=side: edge_copy(side).start())

    def each_other(act):
        def body(off, carry):
            other = lax.rem(me + off, N)
            there_cut, there_tile = other // T, lax.rem(other, T)
            near = jnp.abs(there_tile - tile) <= 1

            @pl.when(near)
            def _():
                act(there_tile, there_cut, off, True)

            @pl.when(jnp.logical_not(near))
            def _():
                act(there_tile, there_cut, off, False)

            return carry

        lax.fori_loop(1, N, body, 0)

    each_other(lambda t, c, off, near: message(t, c, off, near).start())
    here = pl.multiple_of((tile * S + cut) * msg, 8)
    mine = pl.multiple_of((tile * W + lax.rem(cut, W)) * msg, 8)
    got[pl.ds(here, msg), :] = send[pl.ds(mine, msg), :]

    band = lax.broadcasted_iota(jnp.int32, (B, X), 0)
    hop = jnp.zeros((B, X), jnp.float32)
    for b in range(B):
        hop = jnp.where(band == b, hop_ref[b], hop)

    def fill_green(row):
        parts = line_green(edges[row], hop, S)
        for f in range(F):
            for d in range(D):
                green[row, f * D + d] = parts[f][d]
        return parts

    parts = fill_green(1)
    for p in range(NMOM):
        for j in range(HALF):
            wr = 2.0 * math.cos((p + 1) * ANGLES[j]) / PTS
            wi = 2.0 * math.sin((p + 1) * ANGLES[j]) / PTS
            for d in range(D):
                re, im = parts[2 * j][d], parts[2 * j + 1][d]
                final[(p * D + d) * F + 2 * j] = wr * re - wi * im
                final[(p * D + d) * F + 2 * j + 1] = -(wr * im + wi * re)
    for side in (0, 2):

        @pl.when(has_side[side])
        def _(side=side):
            edge_copy(2 - side).wait_recv()
            fill_green(side)

    def arrived(t, c, off, near):
        skip = 0 if near else chunk
        place = got.at[pl.ds(pl.multiple_of((t * S + c) * msg + skip, 8), msg - skip), :]
        pltpu.make_async_remote_copy(
            src_ref=place,
            dst_ref=place,
            send_sem=send_sem.at[off],
            recv_sem=got_sem.at[t, c],
            device_id=(c, t),
            device_id_type=MESH,
        ).wait_recv()

    each_other(arrived)

    def run(low, high, act):
        def body(off, carry):
            act(off)
            return carry

        lax.fori_loop(low, high, body, 0)

    def test_copy(off, inbound):
        other = lax.rem(cut + off, S)
        landing = pl.multiple_of((other if inbound else cut) * (B * R), 8)
        return pltpu.make_async_remote_copy(
            src_ref=tests.at[own_tests, :],
            dst_ref=tests.at[pl.ds(landing, B * R), :],
            send_sem=test_send.at[off],
            recv_sem=test_sem.at[other if inbound else cut],
            device_id=(other, tile),
            device_id_type=MESH,
        )

    run(1, S, lambda off: test_copy(off, False).start())

    def solve_row(row):
        base = (tile + row - 1) * (S * msg)

        def body(b, carry):
            sums = []
            for i in range(npr):
                line = got[pl.ds(base + i * B + b, S, stride=msg), :]
                pairs = [line]
                for d in range(1, half):
                    pairs.append(pltpu.roll(line, d, 0) + pltpu.roll(line, S - d, 0))
                pairs.append(pltpu.roll(line, half, 0))
                sums.append(pairs)
            for f in range(F):
                totals = [None] * npr
                for d in range(D):
                    factor = green[row, f * D + d, pl.ds(b, 1), :]
                    for i in range(npr):
                        term = factor * sums[i][d]
                        totals[i] = term if totals[i] is None else totals[i] + term
                for i in range(npr):
                    first[row, b, f * npr + i] = totals[i]
            return carry

        lax.fori_loop(0, B, body, 0)

    solve_row(1)
    for side in (0, 2):
        pl.when(has_side[side])(lambda side=side: solve_row(side))

        @pl.when(jnp.logical_not(has_side[side]))
        def _(side=side):
            def clear(b, carry):
                first[side, b] = jnp.zeros_like(first[side, 0])
                return carry

            lax.fori_loop(0, B, clear, 0)

    strain = []
    for k in range(6):
        total = None
        for t in range(T):
            term = got[pl.ds(t * S * msg + chunk + k, S, stride=msg), :]
            total = term if total is None else total + term
        strain.append(total)
    for b in range(B):
        for c in range(b, B):
            total = None
            for k in range(6):
                term = (0.5 * (deform_ref[k, b, c] + deform_ref[k, c, b])) * strain[k]
                total = term if total is None else total + term
            mixer[b, c] = total
            if c != b:
                mixer[c, b] = total

    lanes = lax.broadcasted_iota(jnp.int32, (1, 1, X), 2)
    block = max(1, 8 * 8 // S)
    pieces = F * npr // block

    def couple(step, carry):
        b, piece = step // pieces, lax.rem(step, pieces)
        pick = pl.ds(piece * block, block)
        right = left = stay = None
        for c in range(B):
            u = first[1, c, pick]
            up, down = first[2, c, pick], first[0, c, pick]
            a = cross_ref[0, b, c] * u
            l = cross_ref[0, c, b] * u
            s = mixer[b, c][None] * u + cross_ref[1, b, c] * up + cross_ref[1, c, b] * down
            right = a if right is None else right + a
            left = l if left is None else left + l
            stay = s if stay is None else stay + s
        flat = (block * S, X)
        right = pltpu.roll(right.reshape(flat), X - 1, 1).reshape(block, S, X)
        left = pltpu.roll(left.reshape(flat), 1, 1).reshape(block, S, X)
        stay = stay + jnp.where(lanes < X - 1, right, 0.0) + jnp.where(lanes > 0, left, 0.0)
        second[b, pick] = stay
        return carry

    lax.fori_loop(0, B * pieces, couple, 0)

    def moments(b, carry):
        ys = [[second[b, f * npr + i] for f in range(F)] for i in range(npr)]
        for p in range(NMOM):
            totals = [None] * npr
            for j in range(HALF):
                wr = 2.0 * math.cos((p + 1) * ANGLES[j]) / PTS
                wi = 2.0 * math.sin((p + 1) * ANGLES[j]) / PTS
                for i in range(npr):
                    re, im = (first[1, b, (2 * j + comp) * npr + i] for comp in range(2))
                    term = wr * re - wi * im
                    totals[i] = term if totals[i] is None else totals[i] + term
            for d in range(D):
                zs = [None] * npr
                for f in range(F):
                    factor = final[(p * D + d) * F + f, pl.ds(b, 1), :]
                    for i in range(npr):
                        term = factor * ys[i][f]
                        zs[i] = term if zs[i] is None else zs[i] + term
                for i in range(npr):
                    if d == 0:
                        totals[i] = totals[i] + zs[i]
                    elif d == half:
                        totals[i] = totals[i] + pltpu.roll(zs[i], half, 0)
                    else:
                        turned_z = pltpu.roll(zs[i], d, 0) + pltpu.roll(zs[i], S - d, 0)
                        totals[i] = totals[i] + turned_z
            for i in range(npr):
                back[pl.ds((p * npr + i) * B + b, S, stride=ret), :] = totals[i]
        return carry

    lax.fori_loop(0, B, moments, 0)

    mates = (cut // W) * W
    rank = lax.rem(cut, W)

    def home_copy(off, inbound):
        other = lax.rem(rank + off, W)
        source = pl.multiple_of((mates + other) * ret, 8)
        landing = pl.multiple_of((other if inbound else rank) * kept, 8)
        return pltpu.make_async_remote_copy(
            src_ref=back.at[pl.ds(source, kept), :],
            dst_ref=home.at[pl.ds(landing, kept), :],
            send_sem=back_send.at[off],
            recv_sem=home_sem.at[other if inbound else rank],
            device_id=(mates + other, tile),
            device_id_type=MESH,
        )

    run(1, W, lambda off: home_copy(off, False).start())
    home[pl.ds(pl.multiple_of(rank * kept, 8), kept), :] = back[
        pl.ds(pl.multiple_of(cut * ret, 8), kept), :
    ]

    run(1, S, lambda off: test_copy(off, True).wait_recv())

    def halves(values):
        high = values.astype(jnp.bfloat16)
        return high, (values - high.astype(jnp.float32)).astype(jnp.bfloat16)

    def product(left, right):
        return lax.dot_general(
            left, right, (((1,), (1,)), ((), ())), preferred_element_type=jnp.float32
        )

    def project(s, acc):
        high, low = halves(back[pl.ds(pl.multiple_of(s * ret, 8), ret), :])
        test_high, test_low = halves(tests[pl.ds(pl.multiple_of(s * (B * R), 8), B * R), :])
        small = product(high, test_low) + product(low, test_high)
        return acc + (small + product(high, test_high))

    acc = lax.fori_loop(0, S, project, jnp.zeros((ret, B * R), jnp.float32))
    acc = acc.reshape(NMOM * npr, B, B * R)
    lane_band = lax.broadcasted_iota(jnp.int32, acc.shape, 2) // R
    same = lane_band == lax.broadcasted_iota(jnp.int32, acc.shape, 1)
    acc = jnp.sum(jnp.where(same, acc, 0.0), axis=1)
    total = acc
    for b in range(1, B):
        total = total + pltpu.roll(acc, b * R, 1)
    lane_row = lax.broadcasted_iota(jnp.int32, total.shape, 1) // R
    chosen = lane_row == lax.broadcasted_iota(jnp.int32, total.shape, 0)
    total = jnp.sum(jnp.where(chosen, total, 0.0), axis=0, keepdims=True)
    parts_all[me] = total * ((S * B * T * X) ** (-0.5))

    def part_copy(off, inbound):
        other = lax.rem(me + off, N)
        return pltpu.make_async_remote_copy(
            src_ref=parts_all.at[me],
            dst_ref=parts_all.at[other if inbound else me],
            send_sem=part_send.at[off],
            recv_sem=part_sem.at[other if inbound else me],
            device_id=(other // T, lax.rem(other, T)),
            device_id_type=MESH,
        )

    run(1, N, lambda off: part_copy(off, False).start())

    run(1, W, lambda off: home_copy(off, True).wait_recv())
    for w in range(W):
        for p in range(NFIELD):
            for i in range(npr):
                row = w * kept + (p * npr + i) * B
                field_ref[pl.ds(p * B * R + w * npr + i, B, stride=R), :] = home[row : row + B, :]

    each_other(lambda t, c, off, near: message(t, c, off, near).wait_send())
    for side in (0, 2):
        pl.when(has_side[side])(lambda side=side: edge_copy(side).wait_send())
    run(1, S, lambda off: test_copy(off, False).wait_send())
    run(1, W, lambda off: home_copy(off, False).wait_send())
    run(1, N, lambda off: part_copy(off, True).wait_recv())
    for w in range(W):
        total = parts_all[w * T]
        for t in range(1, T):
            total = total + parts_all[w * T + t]
        proj_ref[w : w + 1, :] = total
    run(1, N, lambda off: part_copy(off, False).wait_send())


def on_device(
    S, T, probes, test_block, band_edge, slice_hop, cross_hop, deform, strain_elastic, strain_ids
):
    _, B, R, _, X = probes.shape
    NS, SC = strain_elastic.shape[1], strain_elastic.shape[3]
    dims = (S, T, B, R, X, NS, SC)
    W = min(S, R)
    npr = R // W
    D = S // 2 + 1
    F = 2 * HALF
    chunk = npr * B
    msg = chunk + 8
    ret = NMOM * chunk
    kept = NFIELD * chunk
    hbm = pl.BlockSpec(memory_space=pltpu.HBM)
    vmem = pl.BlockSpec(memory_space=pltpu.VMEM)
    f32 = jnp.float32
    dma = pltpu.SemaphoreType.DMA
    fields, proj = pl.pallas_call(
        functools.partial(kernel, dims),
        out_shape=(
            jax.ShapeDtypeStruct((NFIELD * B * R, X), f32),
            jax.ShapeDtypeStruct((W, B * R), f32),
        ),
        in_specs=[hbm] * 8,
        out_specs=(vmem, vmem),
        scratch_shapes=[
            pltpu.SMEM(strain_ids.shape, jnp.int32),
            pltpu.SMEM(slice_hop.shape, f32),
            pltpu.SMEM(cross_hop.shape, f32),
            pltpu.SMEM(deform.shape, f32),
            pltpu.VMEM((B * R, X), f32),
            pltpu.VMEM((6, NS, SC), f32),
            pltpu.VMEM((S * B * R, X), f32),
            pltpu.VMEM((8, X), f32),
            pltpu.VMEM((T * W * msg, X), f32),
            pltpu.VMEM((T * S * msg, X), f32),
            pltpu.VMEM((3, B, X), f32),
            pltpu.VMEM((3, F * D, B, X), f32),
            pltpu.VMEM((B, B, S, X), f32),
            pltpu.VMEM((3, B, F * npr, S, X), f32),
            pltpu.VMEM((B, F * npr, S, X), f32),
            pltpu.VMEM((S * ret, X), f32),
            pltpu.VMEM((W * kept, X), f32),
            pltpu.VMEM((NMOM * D * F, B, X), f32),
            pltpu.VMEM((S * T, 1, B * R), f32),
            dma((8,)),
            dma((S * T,)),
            dma((T, S)),
            dma((3,)),
            dma((3,)),
            dma((W,)),
            dma((W,)),
            dma((S,)),
            dma((S,)),
            dma((S * T,)),
            dma((S * T,)),
        ],
        compiler_params=pltpu.CompilerParams(
            collective_id=0, has_side_effects=True, vmem_limit_bytes=63 * 1024 * 1024
        ),
    )(
        strain_ids,
        slice_hop,
        cross_hop,
        deform,
        probes.reshape(B * R, X),
        test_block.reshape(B * R, X),
        band_edge.reshape(B, X),
        jnp.transpose(strain_elastic[0], (1, 0, 2)),
    )
    fields = fields.reshape(NFIELD, 1, 1, B, R, 1, X)
    fields = jnp.concatenate([fields, jnp.zeros_like(fields)], axis=1)
    proj = proj[:, : NMOM * npr * R].reshape(W, NMOM, npr, R)
    proj = jnp.transpose(proj, (1, 3, 0, 2)).reshape(NMOM, 1, R, R)
    return fields, jnp.concatenate([proj, jnp.zeros_like(proj)], axis=1)


def solution(mesh):
    placed = (
        P("cuts", None, None, "tile", None),
        P("cuts", None, None, "tile", None),
        P(None, "tile", None),
        P(),
        P(),
        P(),
        P("cuts", "tile", None, None),
        P(),
    )
    return jax.shard_map(
        functools.partial(on_device, mesh.shape["cuts"], mesh.shape["tile"]),
        mesh=mesh,
        in_specs=placed,
        out_specs=(P(None, None, "cuts", None, None, "tile", None), P()),
        check_vma=False,
    )
```

```python
import functools
import math

import jax
import jax.numpy as jnp
import numpy as np
from jax import lax
from jax.experimental import pallas as pl
from jax.experimental.pallas import tpu as pltpu
from jax.sharding import PartitionSpec as P

PTS = 8
HALF = PTS // 2
NMOM = 4
NFIELD = 2
MESH = pl.DeviceIdType.MESH

ANGLES = [math.pi * (2 * point + 1) / PTS for point in range(HALF)]


def line_green(edge, hop, length):
    half = length // 2
    parts = []
    for angle in ANGLES:
        zr, zi = math.cos(angle), math.sin(angle)
        modes = []
        for k in range(half + 1):
            shifted = (zr - edge) + (2.0 * math.cos(2 * math.pi * k / length)) * hop
            inverse = 1.0 / (shifted * shifted + zi * zi)
            modes.append((shifted * inverse, (-zi) * inverse))
        for comp in range(2):
            rows = []
            for d in range(half + 1):
                total = None
                for k in range(half + 1):
                    weight = (1.0 if k in (0, half) else 2.0) / length
                    term = modes[k][comp] * (weight * math.cos(2 * math.pi * k * d / length))
                    total = term if total is None else total + term
                rows.append(total)
            parts.append(rows)
    return parts


def kernel(
    dims,
    ids_in,
    hop_in,
    cross_in,
    deform_in,
    probe_in,
    test_in,
    edge_in,
    elastic_in,
    field_ref,
    proj_ref,
    ids_ref,
    hop_ref,
    cross_ref,
    deform_ref,
    probe_ref,
    elastic_ref,
    tests,
    slots,
    send,
    got,
    edges,
    green,
    mixer,
    first,
    second,
    back,
    home,
    final,
    parts_all,
    load_sem,
    send_sem,
    got_sem,
    edge_send,
    edge_sem,
    back_send,
    home_sem,
    test_send,
    test_sem,
    part_send,
    part_sem,
):
    S, T, B, R, X, NS, SC = dims
    W = min(S, R)
    npr = R // W
    half = S // 2
    D = half + 1
    F = 2 * HALF
    chunk = npr * B
    msg = chunk + 8
    ret = NMOM * chunk
    kept = NFIELD * chunk
    N = S * T
    cut = lax.axis_index("cuts")
    tile = lax.axis_index("tile")
    me = cut * T + tile

    own_tests = pl.ds(pl.multiple_of(cut * (B * R), 8), B * R)
    loads = [
        pltpu.make_async_copy(src, dst, load_sem.at[n])
        for n, (src, dst) in enumerate(
            (
                (probe_in, probe_ref),
                (elastic_in, elastic_ref),
                (ids_in, ids_ref),
                (edge_in, edges.at[1]),
                (hop_in, hop_ref),
                (cross_in, cross_ref),
                (deform_in, deform_ref),
                (test_in, tests.at[own_tests, :]),
            )
        )
    ]
    for load in loads:
        load.start()
    barrier = pltpu.get_barrier_semaphore()

    def others(act):
        for there_tile in range(T):

            def body(off, carry, there_tile=there_tile):
                act(there_tile, lax.rem(cut + off, S))
                return carry

            lax.fori_loop(jnp.where(tile == there_tile, 1, 0), S, body, 0)

    others(
        lambda t, c: pl.semaphore_signal(barrier, inc=1, device_id=(c, t), device_id_type=MESH)
    )

    slots[...] = jnp.zeros_like(slots)
    for load in loads[:3]:
        load.wait()
    for k in range(6):
        for i in range(NS):
            slots[k : k + 1, i * SC : (i + 1) * SC] = elastic_ref[k, i : i + 1, :]
    held = slots[...]
    turned = [held] + [pltpu.roll(held, SC * d, 1) for d in range(1, NS)]
    lane = lax.broadcasted_iota(jnp.int32, (8, X), 1)
    group = lane // SC
    own_ids = [ids_ref[tile * NS + i] for i in range(NS)]
    for t in range(T):
        placed = jnp.zeros((8, X), jnp.float32)
        for i in range(NS):
            for g in range(NS):
                wanted = jnp.where(group == g, t * NS + g, -1)
                placed = jnp.where(wanted == own_ids[i], turned[(g - i) % NS], placed)
        for w in range(W):
            row = (t * W + w) * msg
            for i in range(npr):
                send[row + i * B : row + (i + 1) * B, :] = probe_ref[
                    pl.ds(w * npr + i, B, stride=R), :
                ]
            send[row + chunk : row + msg, :] = placed
    for load in loads[3:]:
        load.wait()

    pl.semaphore_wait(barrier, N - 1)

    def message(target_tile, target_cut, near):
        source = (target_tile * W + lax.rem(target_cut, W)) * msg
        landing = (tile * S + cut) * msg
        skip = 0 if near else chunk
        return pltpu.make_async_remote_copy(
            src_ref=send.at[pl.ds(pl.multiple_of(source + skip, 8), msg - skip), :],
            dst_ref=got.at[pl.ds(pl.multiple_of(landing + skip, 8), msg - skip), :],
            send_sem=send_sem.at[0],
            recv_sem=got_sem.at[tile],
            device_id=(target_cut, target_tile),
            device_id_type=MESH,
        )

    def edge_copy(side):
        return pltpu.make_async_remote_copy(
            src_ref=edges.at[1],
            dst_ref=edges.at[2 - side],
            send_sem=edge_send.at[side],
            recv_sem=edge_sem.at[2 - side],
            device_id=(cut, tile + side - 1),
            device_id_type=MESH,
        )

    has_side = {0: tile > 0, 2: tile < T - 1}
    for side in (0, 2):
        pl.when(has_side[side])(lambda side=side: edge_copy(side).start())

    for there in range(T):
        near = jnp.abs(tile - there) <= 1
        low = jnp.where(tile == there, 1, 0)

        def pushes(near, there=there, low=low):
            def body(off, carry):
                message(there, lax.rem(cut + off, S), near).start()
                return carry

            lax.fori_loop(low, S, body, 0)

        pl.when(near)(lambda pushes=pushes: pushes(True))
        pl.when(jnp.logical_not(near))(lambda pushes=pushes: pushes(False))

    def awaited(ref, send, recv):
        return pltpu.make_async_remote_copy(
            src_ref=ref,
            dst_ref=ref,
            send_sem=send,
            recv_sem=recv,
            device_id=(cut, tile),
            device_id_type=MESH,
        )

    def settle(act):
        for there in range(T):
            gap = jnp.abs(tile - there)
            for wanted, rows in (
                (gap == 0, (S - 1) * msg),
                (gap == 1, S * msg),
                (gap > 1, S * (msg - chunk)),
            ):
                place = got.at[pl.ds(there * S * msg, rows), :]
                pl.when(wanted)(
                    lambda place=place, there=there: act(
                        awaited(place, send_sem.at[0], got_sem.at[there])
                    )
                )

    here = pl.multiple_of((tile * S + cut) * msg, 8)
    mine = pl.multiple_of((tile * W + lax.rem(cut, W)) * msg, 8)
    got[pl.ds(here, msg), :] = send[pl.ds(mine, msg), :]

    band = lax.broadcasted_iota(jnp.int32, (B, X), 0)
    hop = jnp.zeros((B, X), jnp.float32)
    for b in range(B):
        hop = jnp.where(band == b, hop_ref[b], hop)

    def fill_green(row):
        parts = line_green(edges[row], hop, S)
        for f in range(F):
            for d in range(D):
                green[row, f * D + d] = parts[f][d]
        return parts

    parts = fill_green(1)
    for p in range(NMOM):
        for j in range(HALF):
            wr = 2.0 * math.cos((p + 1) * ANGLES[j]) / PTS
            wi = 2.0 * math.sin((p + 1) * ANGLES[j]) / PTS
            for d in range(D):
                re, im = parts[2 * j][d], parts[2 * j + 1][d]
                final[(p * D + d) * F + 2 * j] = wr * re - wi * im
                final[(p * D + d) * F + 2 * j + 1] = -(wr * im + wi * re)
    for side in (0, 2):

        @pl.when(has_side[side])
        def _(side=side):
            edge_copy(2 - side).wait_recv()
            fill_green(side)

    settle(lambda copy: copy.wait_recv())

    def run(low, high, act):
        def body(off, carry):
            act(off)
            return carry

        lax.fori_loop(low, high, body, 0)

    def test_copy(off):
        other = lax.rem(cut + off, S)
        return pltpu.make_async_remote_copy(
            src_ref=tests.at[own_tests, :],
            dst_ref=tests.at[own_tests, :],
            send_sem=test_send.at[0],
            recv_sem=test_sem.at[0],
            device_id=(other, tile),
            device_id_type=MESH,
        )

    run(1, S, lambda off: test_copy(off).start())

    def solve_row(row):
        base = (tile + row - 1) * (S * msg)

        def body(b, carry):
            sums = []
            for i in range(npr):
                line = got[pl.ds(base + i * B + b, S, stride=msg), :]
                pairs = [line]
                for d in range(1, half):
                    pairs.append(pltpu.roll(line, d, 0) + pltpu.roll(line, S - d, 0))
                pairs.append(pltpu.roll(line, half, 0))
                sums.append(pairs)
            for f in range(F):
                totals = [None] * npr
                for d in range(D):
                    factor = green[row, f * D + d, pl.ds(b, 1), :]
                    for i in range(npr):
                        term = factor * sums[i][d]
                        totals[i] = term if totals[i] is None else totals[i] + term
                for i in range(npr):
                    first[row, b, f * npr + i] = totals[i]
            return carry

        lax.fori_loop(0, B, body, 0)

    solve_row(1)
    for side in (0, 2):
        pl.when(has_side[side])(lambda side=side: solve_row(side))

        @pl.when(jnp.logical_not(has_side[side]))
        def _(side=side):
            def clear(b, carry):
                first[side, b] = jnp.zeros_like(first[side, 0])
                return carry

            lax.fori_loop(0, B, clear, 0)

    strain = []
    for k in range(6):
        total = None
        for t in range(T):
            term = got[pl.ds(t * S * msg + chunk + k, S, stride=msg), :]
            total = term if total is None else total + term
        strain.append(total)
    for b in range(B):
        for c in range(b, B):
            total = None
            for k in range(6):
                term = (0.5 * (deform_ref[k, b, c] + deform_ref[k, c, b])) * strain[k]
                total = term if total is None else total + term
            mixer[b, c] = total
            if c != b:
                mixer[c, b] = total

    lanes = lax.broadcasted_iota(jnp.int32, (1, 1, X), 2)
    block = max(1, 8 * 8 // S)
    pieces = F * npr // block

    def couple(step, carry):
        b, piece = step // pieces, lax.rem(step, pieces)
        pick = pl.ds(piece * block, block)
        right = left = stay = None
        for c in range(B):
            u = first[1, c, pick]
            up, down = first[2, c, pick], first[0, c, pick]
            a = cross_ref[0, b, c] * u
            l = cross_ref[0, c, b] * u
            s = mixer[b, c][None] * u + cross_ref[1, b, c] * up + cross_ref[1, c, b] * down
            right = a if right is None else right + a
            left = l if left is None else left + l
            stay = s if stay is None else stay + s
        flat = (block * S, X)
        right = pltpu.roll(right.reshape(flat), X - 1, 1).reshape(block, S, X)
        left = pltpu.roll(left.reshape(flat), 1, 1).reshape(block, S, X)
        stay = stay + jnp.where(lanes < X - 1, right, 0.0) + jnp.where(lanes > 0, left, 0.0)
        second[b, pick] = stay
        return carry

    lax.fori_loop(0, B * pieces, couple, 0)

    def moments(b, carry):
        ys = [[second[b, f * npr + i] for f in range(F)] for i in range(npr)]
        for p in range(NMOM):
            totals = [None] * npr
            for j in range(HALF):
                wr = 2.0 * math.cos((p + 1) * ANGLES[j]) / PTS
                wi = 2.0 * math.sin((p + 1) * ANGLES[j]) / PTS
                for i in range(npr):
                    re, im = (first[1, b, (2 * j + comp) * npr + i] for comp in range(2))
                    term = wr * re - wi * im
                    totals[i] = term if totals[i] is None else totals[i] + term
            for d in range(D):
                zs = [None] * npr
                for f in range(F):
                    factor = final[(p * D + d) * F + f, pl.ds(b, 1), :]
                    for i in range(npr):
                        term = factor * ys[i][f]
                        zs[i] = term if zs[i] is None else zs[i] + term
                for i in range(npr):
                    if d == 0:
                        totals[i] = totals[i] + zs[i]
                    elif d == half:
                        totals[i] = totals[i] + pltpu.roll(zs[i], half, 0)
                    else:
                        turned_z = pltpu.roll(zs[i], d, 0) + pltpu.roll(zs[i], S - d, 0)
                        totals[i] = totals[i] + turned_z
            for i in range(npr):
                back[pl.ds((p * npr + i) * B + b, S, stride=ret), :] = totals[i]
        return carry

    lax.fori_loop(0, B, moments, 0)

    mates = (cut // W) * W
    rank = lax.rem(cut, W)

    landing = pl.multiple_of(rank * kept, 8)

    def home_copy(off):
        other = lax.rem(rank + off, W)
        source = pl.multiple_of((mates + other) * ret, 8)
        return pltpu.make_async_remote_copy(
            src_ref=back.at[pl.ds(source, kept), :],
            dst_ref=home.at[pl.ds(landing, kept), :],
            send_sem=back_send.at[0],
            recv_sem=home_sem.at[0],
            device_id=(mates + other, tile),
            device_id_type=MESH,
        )

    run(1, W, lambda off: home_copy(off).start())
    home[pl.ds(landing, kept), :] = back[
        pl.ds(pl.multiple_of(cut * ret, 8), kept), :
    ]

    all_tests = awaited(tests.at[pl.ds(0, (S - 1) * B * R), :], test_send.at[0], test_sem.at[0])
    all_tests.wait_recv()

    def halves(values):
        high = values.astype(jnp.bfloat16)
        return high, (values - high.astype(jnp.float32)).astype(jnp.bfloat16)

    def product(left, right):
        return lax.dot_general(
            left, right, (((1,), (1,)), ((), ())), preferred_element_type=jnp.float32
        )

    def by_slice(ref, rows):
        return halves(
            jnp.concatenate([ref[s * rows : (s + 1) * rows, :] for s in range(S)], axis=1)
        )

    high, low = by_slice(back, ret)
    test_high, test_low = by_slice(tests, B * R)
    acc = product(high, test_low) + product(low, test_high) + product(high, test_high)
    acc = acc.reshape(NMOM * npr, B, B * R)
    lane_band = lax.broadcasted_iota(jnp.int32, acc.shape, 2) // R
    same = lane_band == lax.broadcasted_iota(jnp.int32, acc.shape, 1)
    acc = jnp.sum(jnp.where(same, acc, 0.0), axis=1)
    total = acc
    for b in range(1, B):
        total = total + pltpu.roll(acc, b * R, 1)
    lane_row = lax.broadcasted_iota(jnp.int32, total.shape, 1) // R
    chosen = lane_row == lax.broadcasted_iota(jnp.int32, total.shape, 0)
    total = jnp.sum(jnp.where(chosen, total, 0.0), axis=0, keepdims=True)
    parts_all[me] = total * ((S * B * T * X) ** (-0.5))

    def part_copy(there_tile, there_cut):
        return pltpu.make_async_remote_copy(
            src_ref=parts_all.at[me],
            dst_ref=parts_all.at[me],
            send_sem=part_send.at[0],
            recv_sem=part_sem.at[0],
            device_id=(there_cut, there_tile),
            device_id_type=MESH,
        )

    others(lambda t, c: part_copy(t, c).start())

    all_home = awaited(home.at[pl.ds(0, (W - 1) * kept), :], back_send.at[0], home_sem.at[0])
    all_home.wait_recv()
    for w in range(W):
        for p in range(NFIELD):
            for i in range(npr):
                row = w * kept + (p * npr + i) * B
                field_ref[pl.ds(p * B * R + w * npr + i, B, stride=R), :] = home[row : row + B, :]

    settle(lambda copy: copy.wait_send())
    for side in (0, 2):
        pl.when(has_side[side])(lambda side=side: edge_copy(side).wait_send())
    all_tests.wait_send()
    all_home.wait_send()
    all_parts = awaited(parts_all.at[pl.ds(0, N - 1)], part_send.at[0], part_sem.at[0])
    all_parts.wait_recv()
    for w in range(W):
        total = parts_all[w * T]
        for t in range(1, T):
            total = total + parts_all[w * T + t]
        proj_ref[w : w + 1, :] = total
    all_parts.wait_send()


def on_device(
    S, T, probes, test_block, band_edge, slice_hop, cross_hop, deform, strain_elastic, strain_ids
):
    _, B, R, _, X = probes.shape
    NS, SC = strain_elastic.shape[1], strain_elastic.shape[3]
    dims = (S, T, B, R, X, NS, SC)
    W = min(S, R)
    npr = R // W
    D = S // 2 + 1
    F = 2 * HALF
    chunk = npr * B
    msg = chunk + 8
    ret = NMOM * chunk
    kept = NFIELD * chunk
    hbm = pl.BlockSpec(memory_space=pltpu.HBM)
    vmem = pl.BlockSpec(memory_space=pltpu.VMEM)
    f32 = jnp.float32
    dma = pltpu.SemaphoreType.DMA
    fields, proj = pl.pallas_call(
        functools.partial(kernel, dims),
        out_shape=(
            jax.ShapeDtypeStruct((NFIELD * B * R, X), f32),
            jax.ShapeDtypeStruct((W, B * R), f32),
        ),
        in_specs=[hbm] * 8,
        out_specs=(vmem, vmem),
        scratch_shapes=[
            pltpu.SMEM(strain_ids.shape, jnp.int32),
            pltpu.SMEM(slice_hop.shape, f32),
            pltpu.SMEM(cross_hop.shape, f32),
            pltpu.SMEM(deform.shape, f32),
            pltpu.VMEM((B * R, X), f32),
            pltpu.VMEM((6, NS, SC), f32),
            pltpu.VMEM((S * B * R, X), f32),
            pltpu.VMEM((8, X), f32),
            pltpu.VMEM((T * W * msg, X), f32),
            pltpu.VMEM((T * S * msg, X), f32),
            pltpu.VMEM((3, B, X), f32),
            pltpu.VMEM((3, F * D, B, X), f32),
            pltpu.VMEM((B, B, S, X), f32),
            pltpu.VMEM((3, B, F * npr, S, X), f32),
            pltpu.VMEM((B, F * npr, S, X), f32),
            pltpu.VMEM((S * ret, X), f32),
            pltpu.VMEM((W * kept, X), f32),
            pltpu.VMEM((NMOM * D * F, B, X), f32),
            pltpu.VMEM((S * T, 1, B * R), f32),
            dma((8,)),
            dma((1,)),
            dma((T,)),
            dma((3,)),
            dma((3,)),
            dma((1,)),
            dma((1,)),
            dma((1,)),
            dma((1,)),
            dma((1,)),
            dma((1,)),
        ],
        compiler_params=pltpu.CompilerParams(
            collective_id=0, has_side_effects=True, vmem_limit_bytes=63 * 1024 * 1024
        ),
    )(
        strain_ids,
        slice_hop,
        cross_hop,
        deform,
        probes.reshape(B * R, X),
        test_block.reshape(B * R, X),
        band_edge.reshape(B, X),
        jnp.transpose(strain_elastic[0], (1, 0, 2)),
    )
    fields = fields.reshape(NFIELD, 1, 1, B, R, 1, X)
    fields = jnp.concatenate([fields, jnp.zeros_like(fields)], axis=1)
    proj = proj[:, : NMOM * npr * R].reshape(W, NMOM, npr, R)
    proj = jnp.transpose(proj, (1, 3, 0, 2)).reshape(NMOM, 1, R, R)
    return fields, jnp.concatenate([proj, jnp.zeros_like(proj)], axis=1)


def solution(mesh):
    placed = (
        P("cuts", None, None, "tile", None),
        P("cuts", None, None, "tile", None),
        P(None, "tile", None),
        P(),
        P(),
        P(),
        P("cuts", "tile", None, None),
        P(),
    )
    return jax.shard_map(
        functools.partial(on_device, mesh.shape["cuts"], mesh.shape["tile"]),
        mesh=mesh,
        in_specs=placed,
        out_specs=(P(None, None, "cuts", None, None, "tile", None), P()),
        check_vma=False,
    )
```

```python
import functools
import math

import jax
import jax.numpy as jnp
import numpy as np
from jax import lax
from jax.experimental import pallas as pl
from jax.experimental.pallas import tpu as pltpu
from jax.sharding import PartitionSpec as P

PTS = 8
HALF = PTS // 2
NMOM = 4
NFIELD = 2
MESH = pl.DeviceIdType.MESH

ANGLES = [math.pi * (2 * point + 1) / PTS for point in range(HALF)]


def line_green(edge, hop, length):
    half = length // 2
    parts = []
    for angle in ANGLES:
        zr, zi = math.cos(angle), math.sin(angle)
        modes = []
        for k in range(half + 1):
            shifted = (zr - edge) + (2.0 * math.cos(2 * math.pi * k / length)) * hop
            inverse = 1.0 / (shifted * shifted + zi * zi)
            modes.append((shifted * inverse, (-zi) * inverse))
        for comp in range(2):
            rows = []
            for d in range(half + 1):
                total = None
                for k in range(half + 1):
                    weight = (1.0 if k in (0, half) else 2.0) / length
                    term = modes[k][comp] * (weight * math.cos(2 * math.pi * k * d / length))
                    total = term if total is None else total + term
                rows.append(total)
            parts.append(rows)
    return parts


def kernel(
    dims,
    ids_in,
    hop_in,
    cross_in,
    deform_in,
    probe_in,
    test_in,
    edge_in,
    elastic_in,
    field_ref,
    proj_ref,
    ids_ref,
    hop_ref,
    cross_ref,
    deform_ref,
    probe_ref,
    elastic_ref,
    tests,
    slots,
    send,
    got,
    edges,
    green,
    mixer,
    first,
    second,
    back,
    home,
    final,
    parts_all,
    load_sem,
    send_sem,
    got_sem,
    edge_send,
    edge_sem,
    back_send,
    home_sem,
    test_send,
    test_sem,
    part_send,
    part_sem,
):
    S, T, B, R, X, NS, SC = dims
    W = min(S, R)
    npr = R // W
    half = S // 2
    D = half + 1
    F = 2 * HALF
    chunk = npr * B
    msg = chunk + 8
    ret = NMOM * chunk
    kept = NFIELD * chunk
    N = S * T
    cut = lax.axis_index("cuts")
    tile = lax.axis_index("tile")
    me = cut * T + tile

    own_tests = pl.ds(pl.multiple_of(cut * (B * R), 8), B * R)
    loads = [
        pltpu.make_async_copy(src, dst, load_sem.at[n])
        for n, (src, dst) in enumerate(
            (
                (probe_in, probe_ref),
                (elastic_in, elastic_ref),
                (ids_in, ids_ref),
                (edge_in, edges.at[1]),
                (hop_in, hop_ref),
                (cross_in, cross_ref),
                (deform_in, deform_ref),
                (test_in, tests.at[own_tests, :]),
            )
        )
    ]
    for load in loads:
        load.start()
    barrier = pltpu.get_barrier_semaphore()

    def others(act):
        for there_tile in range(T):

            def body(off, carry, there_tile=there_tile):
                act(there_tile, lax.rem(cut + off, S))
                return carry

            lax.fori_loop(jnp.where(tile == there_tile, 1, 0), S, body, 0)

    others(
        lambda t, c: pl.semaphore_signal(barrier, inc=1, device_id=(c, t), device_id_type=MESH)
    )

    slots[...] = jnp.zeros_like(slots)
    for load in loads[:3]:
        load.wait()
    for k in range(6):
        for i in range(NS):
            slots[k : k + 1, i * SC : (i + 1) * SC] = elastic_ref[k, i : i + 1, :]
    held = slots[...]
    turned = [held] + [pltpu.roll(held, SC * d, 1) for d in range(1, NS)]
    lane = lax.broadcasted_iota(jnp.int32, (8, X), 1)
    group = lane // SC
    own_ids = [ids_ref[tile * NS + i] for i in range(NS)]
    for t in range(T):
        placed = jnp.zeros((8, X), jnp.float32)
        for i in range(NS):
            for g in range(NS):
                wanted = jnp.where(group == g, t * NS + g, -1)
                placed = jnp.where(wanted == own_ids[i], turned[(g - i) % NS], placed)
        for w in range(W):
            row = (t * W + w) * msg
            for i in range(npr):
                send[row + i * B : row + (i + 1) * B, :] = probe_ref[
                    pl.ds(w * npr + i, B, stride=R), :
                ]
            send[row + chunk : row + msg, :] = placed
    for load in loads[3:]:
        load.wait()

    pl.semaphore_wait(barrier, N - 1)

    def message(target_tile, target_cut, near):
        source = (target_tile * W + lax.rem(target_cut, W)) * msg
        landing = (tile * S + cut) * msg
        skip = 0 if near else chunk
        return pltpu.make_async_remote_copy(
            src_ref=send.at[pl.ds(pl.multiple_of(source + skip, 8), msg - skip), :],
            dst_ref=got.at[pl.ds(pl.multiple_of(landing + skip, 8), msg - skip), :],
            send_sem=send_sem.at[0],
            recv_sem=got_sem.at[tile],
            device_id=(target_cut, target_tile),
            device_id_type=MESH,
        )

    def edge_copy(side):
        return pltpu.make_async_remote_copy(
            src_ref=edges.at[1],
            dst_ref=edges.at[2 - side],
            send_sem=edge_send.at[side],
            recv_sem=edge_sem.at[2 - side],
            device_id=(cut, tile + side - 1),
            device_id_type=MESH,
        )

    has_side = {0: tile > 0, 2: tile < T - 1}
    for side in (0, 2):
        pl.when(has_side[side])(lambda side=side: edge_copy(side).start())

    for there in range(T):
        near = jnp.abs(tile - there) <= 1
        low = jnp.where(tile == there, 1, 0)

        def pushes(near, there=there, low=low):
            def body(off, carry):
                message(there, lax.rem(cut + off, S), near).start()
                return carry

            lax.fori_loop(low, S, body, 0)

        pl.when(near)(lambda pushes=pushes: pushes(True))
        pl.when(jnp.logical_not(near))(lambda pushes=pushes: pushes(False))

    def awaited(ref, send, recv):
        return pltpu.make_async_remote_copy(
            src_ref=ref,
            dst_ref=ref,
            send_sem=send,
            recv_sem=recv,
            device_id=(cut, tile),
            device_id_type=MESH,
        )

    def settle(act):
        for there in range(T):
            gap = jnp.abs(tile - there)
            for wanted, rows in (
                (gap == 0, (S - 1) * msg),
                (gap == 1, S * msg),
                (gap > 1, S * (msg - chunk)),
            ):
                place = got.at[pl.ds(there * S * msg, rows), :]
                pl.when(wanted)(
                    lambda place=place, there=there: act(
                        awaited(place, send_sem.at[0], got_sem.at[there])
                    )
                )

    here = pl.multiple_of((tile * S + cut) * msg, 8)
    mine = pl.multiple_of((tile * W + lax.rem(cut, W)) * msg, 8)
    got[pl.ds(here, msg), :] = send[pl.ds(mine, msg), :]

    band = lax.broadcasted_iota(jnp.int32, (B, X), 0)
    hop = jnp.zeros((B, X), jnp.float32)
    for b in range(B):
        hop = jnp.where(band == b, hop_ref[b], hop)

    def fill_green(row):
        parts = line_green(edges[row], hop, S)
        for f in range(F):
            for d in range(D):
                green[row, pl.ds(d * F + f, B, stride=D * F), :] = parts[f][d]
        return parts

    parts = fill_green(1)
    for p in range(NMOM):
        for j in range(HALF):
            wr = 2.0 * math.cos((p + 1) * ANGLES[j]) / PTS
            wi = 2.0 * math.sin((p + 1) * ANGLES[j]) / PTS
            for d in range(D):
                re, im = parts[2 * j][d], parts[2 * j + 1][d]
                final[pl.ds((p * D + d) * F + 2 * j, B, stride=NMOM * D * F), :] = wr * re - wi * im
                final[pl.ds((p * D + d) * F + 2 * j + 1, B, stride=NMOM * D * F), :] = -(
                    wr * im + wi * re
                )
    for side in (0, 2):

        @pl.when(has_side[side])
        def _(side=side):
            edge_copy(2 - side).wait_recv()
            fill_green(side)

    settle(lambda copy: copy.wait_recv())

    def run(low, high, act):
        def body(off, carry):
            act(off)
            return carry

        lax.fori_loop(low, high, body, 0)

    def test_copy(off):
        other = lax.rem(cut + off, S)
        return pltpu.make_async_remote_copy(
            src_ref=tests.at[own_tests, :],
            dst_ref=tests.at[own_tests, :],
            send_sem=test_send.at[0],
            recv_sem=test_sem.at[0],
            device_id=(other, tile),
            device_id_type=MESH,
        )

    run(1, S, lambda off: test_copy(off).start())

    def solve_row(row):
        base = (tile + row - 1) * (S * msg)

        def body(b, carry):
            sums = []
            for i in range(npr):
                line = got[pl.ds(base + i * B + b, S, stride=msg), :]
                pairs = [line]
                for d in range(1, half):
                    pairs.append(pltpu.roll(line, d, 0) + pltpu.roll(line, S - d, 0))
                pairs.append(pltpu.roll(line, half, 0))
                sums.append(pairs)
            factors = [
                green[row, pl.ds(pl.multiple_of((b * D + d) * F, 8), F), :] for d in range(D)
            ]
            for f in range(F):
                totals = [None] * npr
                for d in range(D):
                    factor = factors[d][f : f + 1]
                    for i in range(npr):
                        term = factor * sums[i][d]
                        totals[i] = term if totals[i] is None else totals[i] + term
                for i in range(npr):
                    first[row, b, f * npr + i] = totals[i]
            return carry

        lax.fori_loop(0, B, body, 0)

    solve_row(1)
    for side in (0, 2):
        pl.when(has_side[side])(lambda side=side: solve_row(side))

        @pl.when(jnp.logical_not(has_side[side]))
        def _(side=side):
            def clear(b, carry):
                first[side, b] = jnp.zeros_like(first[side, 0])
                return carry

            lax.fori_loop(0, B, clear, 0)

    strain = []
    for k in range(6):
        total = None
        for t in range(T):
            term = got[pl.ds(t * S * msg + chunk + k, S, stride=msg), :]
            total = term if total is None else total + term
        strain.append(total)
    for b in range(B):
        for c in range(b, B):
            total = None
            for k in range(6):
                term = (0.5 * (deform_ref[k, b, c] + deform_ref[k, c, b])) * strain[k]
                total = term if total is None else total + term
            mixer[b, c] = total
            if c != b:
                mixer[c, b] = total

    lanes = lax.broadcasted_iota(jnp.int32, (1, 1, X), 2)
    block = max(1, 8 * 8 // S)
    pieces = F * npr // block

    def couple(step, carry):
        b, piece = step // pieces, lax.rem(step, pieces)
        pick = pl.ds(piece * block, block)
        right = left = stay = None
        for c in range(B):
            u = first[1, c, pick]
            up, down = first[2, c, pick], first[0, c, pick]
            a = cross_ref[0, b, c] * u
            l = cross_ref[0, c, b] * u
            s = mixer[b, c][None] * u + cross_ref[1, b, c] * up + cross_ref[1, c, b] * down
            right = a if right is None else right + a
            left = l if left is None else left + l
            stay = s if stay is None else stay + s
        flat = (block * S, X)
        right = pltpu.roll(right.reshape(flat), X - 1, 1).reshape(block, S, X)
        left = pltpu.roll(left.reshape(flat), 1, 1).reshape(block, S, X)
        stay = stay + jnp.where(lanes < X - 1, right, 0.0) + jnp.where(lanes > 0, left, 0.0)
        second[b, pick] = stay
        return carry

    lax.fori_loop(0, B * pieces, couple, 0)

    def moments(b, carry):
        ys = [[second[b, f * npr + i] for f in range(F)] for i in range(npr)]
        for p in range(NMOM):
            totals = [None] * npr
            for j in range(HALF):
                wr = 2.0 * math.cos((p + 1) * ANGLES[j]) / PTS
                wi = 2.0 * math.sin((p + 1) * ANGLES[j]) / PTS
                for i in range(npr):
                    re, im = (first[1, b, (2 * j + comp) * npr + i] for comp in range(2))
                    term = wr * re - wi * im
                    totals[i] = term if totals[i] is None else totals[i] + term
            for d in range(D):
                zs = [None] * npr
                start = pl.multiple_of(((b * NMOM + p) * D + d) * F, 8)
                factors = final[pl.ds(start, F), :]
                for f in range(F):
                    factor = factors[f : f + 1]
                    for i in range(npr):
                        term = factor * ys[i][f]
                        zs[i] = term if zs[i] is None else zs[i] + term
                for i in range(npr):
                    if d == 0:
                        totals[i] = totals[i] + zs[i]
                    elif d == half:
                        totals[i] = totals[i] + pltpu.roll(zs[i], half, 0)
                    else:
                        turned_z = pltpu.roll(zs[i], d, 0) + pltpu.roll(zs[i], S - d, 0)
                        totals[i] = totals[i] + turned_z
            for i in range(npr):
                back[pl.ds((p * npr + i) * B + b, S, stride=ret), :] = totals[i]
        return carry

    lax.fori_loop(0, B, moments, 0)

    mates = (cut // W) * W
    rank = lax.rem(cut, W)

    landing = pl.multiple_of(rank * kept, 8)

    def home_copy(off):
        other = lax.rem(rank + off, W)
        source = pl.multiple_of((mates + other) * ret, 8)
        return pltpu.make_async_remote_copy(
            src_ref=back.at[pl.ds(source, kept), :],
            dst_ref=home.at[pl.ds(landing, kept), :],
            send_sem=back_send.at[0],
            recv_sem=home_sem.at[0],
            device_id=(mates + other, tile),
            device_id_type=MESH,
        )

    run(1, W, lambda off: home_copy(off).start())
    home[pl.ds(landing, kept), :] = back[
        pl.ds(pl.multiple_of(cut * ret, 8), kept), :
    ]

    all_tests = awaited(tests.at[pl.ds(0, (S - 1) * B * R), :], test_send.at[0], test_sem.at[0])
    all_tests.wait_recv()

    def halves(values):
        high = values.astype(jnp.bfloat16)
        return high, (values - high.astype(jnp.float32)).astype(jnp.bfloat16)

    def product(left, right):
        return lax.dot_general(
            left, right, (((1,), (1,)), ((), ())), preferred_element_type=jnp.float32
        )

    def by_slice(ref, rows):
        return halves(
            jnp.concatenate([ref[s * rows : (s + 1) * rows, :] for s in range(S)], axis=1)
        )

    high, low = by_slice(back, ret)
    test_high, test_low = by_slice(tests, B * R)
    acc = product(high, test_low) + product(low, test_high) + product(high, test_high)
    acc = acc.reshape(NMOM * npr, B, B * R)
    lane_band = lax.broadcasted_iota(jnp.int32, acc.shape, 2) // R
    same = lane_band == lax.broadcasted_iota(jnp.int32, acc.shape, 1)
    acc = jnp.sum(jnp.where(same, acc, 0.0), axis=1)
    total = acc
    for b in range(1, B):
        total = total + pltpu.roll(acc, b * R, 1)
    lane_row = lax.broadcasted_iota(jnp.int32, total.shape, 1) // R
    chosen = lane_row == lax.broadcasted_iota(jnp.int32, total.shape, 0)
    total = jnp.sum(jnp.where(chosen, total, 0.0), axis=0, keepdims=True)
    parts_all[me] = total * ((S * B * T * X) ** (-0.5))

    def part_copy(there_tile, there_cut):
        return pltpu.make_async_remote_copy(
            src_ref=parts_all.at[me],
            dst_ref=parts_all.at[me],
            send_sem=part_send.at[0],
            recv_sem=part_sem.at[0],
            device_id=(there_cut, there_tile),
            device_id_type=MESH,
        )

    others(lambda t, c: part_copy(t, c).start())

    all_home = awaited(home.at[pl.ds(0, (W - 1) * kept), :], back_send.at[0], home_sem.at[0])
    all_home.wait_recv()
    for w in range(W):
        for p in range(NFIELD):
            for i in range(npr):
                row = w * kept + (p * npr + i) * B
                field_ref[pl.ds(p * B * R + w * npr + i, B, stride=R), :] = home[row : row + B, :]

    settle(lambda copy: copy.wait_send())
    for side in (0, 2):
        pl.when(has_side[side])(lambda side=side: edge_copy(side).wait_send())
    all_tests.wait_send()
    all_home.wait_send()
    all_parts = awaited(parts_all.at[pl.ds(0, N - 1)], part_send.at[0], part_sem.at[0])
    all_parts.wait_recv()
    for w in range(W):
        total = parts_all[w * T]
        for t in range(1, T):
            total = total + parts_all[w * T + t]
        proj_ref[w : w + 1, :] = total
    all_parts.wait_send()


def emit(npr, field_in, proj_in, field_out, proj_out, zeros, held, sems):
    W, columns = held.shape
    R = proj_out.shape[-1]
    load = pltpu.make_async_copy(proj_in, held, sems.at[0])
    load.start()
    copies = []
    for p in range(NFIELD):
        copies.append(
            pltpu.make_async_copy(field_in.at[p], field_out.at[p, 0], sems.at[1 + 2 * p])
        )
        copies[-1].start()
    zeros[...] = jnp.zeros_like(zeros)
    for p in range(NFIELD):
        copies.append(pltpu.make_async_copy(zeros, field_out.at[p, 1], sems.at[2 + 2 * p]))
        copies[-1].start()
    load.wait()
    turned = jnp.transpose(held[...])
    worker = lax.broadcasted_iota(jnp.int32, (W, R), 0) * npr
    column = lax.broadcasted_iota(jnp.int32, (W, R), 1)
    spread = []
    for i in range(npr):
        placing = jnp.where(column == worker + i, 1.0, 0.0)
        spread.append(jnp.dot(turned, placing, precision=lax.Precision.HIGHEST))
    for p in range(NMOM):
        total = None
        for i in range(npr):
            row = (p * npr + i) * R
            term = spread[i][row : row + R]
            total = term if total is None else total + term
        proj_out[p, 0] = total
        proj_out[p, 1] = jnp.zeros_like(total)
    for copy in copies:
        copy.wait()


def on_device(
    S, T, probes, test_block, band_edge, slice_hop, cross_hop, deform, strain_elastic, strain_ids
):
    _, B, R, _, X = probes.shape
    NS, SC = strain_elastic.shape[1], strain_elastic.shape[3]
    dims = (S, T, B, R, X, NS, SC)
    W = min(S, R)
    npr = R // W
    D = S // 2 + 1
    F = 2 * HALF
    chunk = npr * B
    msg = chunk + 8
    ret = NMOM * chunk
    kept = NFIELD * chunk
    hbm = pl.BlockSpec(memory_space=pltpu.HBM)
    vmem = pl.BlockSpec(memory_space=pltpu.VMEM)
    f32 = jnp.float32
    dma = pltpu.SemaphoreType.DMA
    fields, proj = pl.pallas_call(
        functools.partial(kernel, dims),
        out_shape=(
            jax.ShapeDtypeStruct((NFIELD * B * R, X), f32),
            jax.ShapeDtypeStruct((W, B * R), f32),
        ),
        in_specs=[hbm] * 8,
        out_specs=(vmem, vmem),
        scratch_shapes=[
            pltpu.SMEM(strain_ids.shape, jnp.int32),
            pltpu.SMEM(slice_hop.shape, f32),
            pltpu.SMEM(cross_hop.shape, f32),
            pltpu.SMEM(deform.shape, f32),
            pltpu.VMEM((B * R, X), f32),
            pltpu.VMEM((6, NS, SC), f32),
            pltpu.VMEM((S * B * R, X), f32),
            pltpu.VMEM((8, X), f32),
            pltpu.VMEM((T * W * msg, X), f32),
            pltpu.VMEM((T * S * msg, X), f32),
            pltpu.VMEM((3, B, X), f32),
            pltpu.VMEM((3, B * D * F, X), f32),
            pltpu.VMEM((B, B, S, X), f32),
            pltpu.VMEM((3, B, F * npr, S, X), f32),
            pltpu.VMEM((B, F * npr, S, X), f32),
            pltpu.VMEM((S * ret, X), f32),
            pltpu.VMEM((W * kept, X), f32),
            pltpu.VMEM((B * NMOM * D * F, X), f32),
            pltpu.VMEM((S * T, 1, B * R), f32),
            dma((8,)),
            dma((1,)),
            dma((T,)),
            dma((3,)),
            dma((3,)),
            dma((1,)),
            dma((1,)),
            dma((1,)),
            dma((1,)),
            dma((1,)),
            dma((1,)),
        ],
        compiler_params=pltpu.CompilerParams(
            collective_id=0, has_side_effects=True, vmem_limit_bytes=63 * 1024 * 1024
        ),
    )(
        strain_ids,
        slice_hop,
        cross_hop,
        deform,
        probes.reshape(B * R, X),
        test_block.reshape(B * R, X),
        band_edge.reshape(B, X),
        jnp.transpose(strain_elastic[0], (1, 0, 2)),
    )
    fields, proj = pl.pallas_call(
        functools.partial(emit, npr),
        out_shape=(
            jax.ShapeDtypeStruct((NFIELD, 2, B * R, X), f32),
            jax.ShapeDtypeStruct((NMOM, 2, R, R), f32),
        ),
        in_specs=[hbm] * 2,
        out_specs=(hbm, vmem),
        scratch_shapes=[
            pltpu.VMEM((B * R, X), f32),
            pltpu.VMEM((W, B * R), f32),
            dma((1 + 2 * NFIELD,)),
        ],
        compiler_params=pltpu.CompilerParams(vmem_limit_bytes=63 * 1024 * 1024),
    )(fields.reshape(NFIELD, B * R, X), proj)
    return fields.reshape(NFIELD, 2, 1, B, R, 1, X), proj


def solution(mesh):
    placed = (
        P("cuts", None, None, "tile", None),
        P("cuts", None, None, "tile", None),
        P(None, "tile", None),
        P(),
        P(),
        P(),
        P("cuts", "tile", None, None),
        P(),
    )
    return jax.shard_map(
        functools.partial(on_device, mesh.shape["cuts"], mesh.shape["tile"]),
        mesh=mesh,
        in_specs=placed,
        out_specs=(P(None, None, "cuts", None, None, "tile", None), P()),
        check_vma=False,
    )
```

```python
import functools
import math

import jax
import jax.numpy as jnp
import numpy as np
from jax import lax
from jax.experimental import pallas as pl
from jax.experimental.pallas import tpu as pltpu
from jax.sharding import PartitionSpec as P

PTS = 8
HALF = PTS // 2
NMOM = 4
NFIELD = 2
MESH = pl.DeviceIdType.MESH

ANGLES = [math.pi * (2 * point + 1) / PTS for point in range(HALF)]


def line_green(edge, hop, length):
    half = length // 2
    parts = []
    for angle in ANGLES:
        zr, zi = math.cos(angle), math.sin(angle)
        modes = []
        for k in range(half + 1):
            shifted = (zr - edge) + (2.0 * math.cos(2 * math.pi * k / length)) * hop
            inverse = 1.0 / (shifted * shifted + zi * zi)
            modes.append((shifted * inverse, (-zi) * inverse))
        for comp in range(2):
            rows = []
            for d in range(half + 1):
                total = None
                for k in range(half + 1):
                    weight = (1.0 if k in (0, half) else 2.0) / length
                    term = modes[k][comp] * (weight * math.cos(2 * math.pi * k * d / length))
                    total = term if total is None else total + term
                rows.append(total)
            parts.append(rows)
    return parts


def kernel(
    dims,
    ids_in,
    hop_in,
    cross_in,
    deform_in,
    probe_in,
    test_in,
    edge_in,
    elastic_in,
    field_ref,
    proj_ref,
    ids_ref,
    hop_ref,
    cross_ref,
    deform_ref,
    probe_ref,
    elastic_ref,
    tests,
    slots,
    send,
    got,
    edges,
    green,
    mixer,
    first,
    second,
    back,
    home,
    final,
    parts_all,
    load_sem,
    send_sem,
    got_sem,
    edge_send,
    edge_sem,
    back_send,
    home_sem,
    test_send,
    test_sem,
    part_send,
    part_sem,
):
    S, T, B, R, X, NS, SC = dims
    W = min(S, R)
    npr = R // W
    half = S // 2
    D = half + 1
    F = 2 * HALF
    chunk = npr * B
    msg = chunk + 8
    ret = NMOM * chunk
    kept = NFIELD * chunk
    N = S * T
    cut = lax.axis_index("cuts")
    tile = lax.axis_index("tile")
    me = cut * T + tile

    own_tests = pl.ds(pl.multiple_of(cut * (B * R), 8), B * R)
    loads = [
        pltpu.make_async_copy(src, dst, load_sem.at[n])
        for n, (src, dst) in enumerate(
            (
                (probe_in, probe_ref),
                (elastic_in, elastic_ref),
                (ids_in, ids_ref),
                (edge_in, edges.at[1]),
                (hop_in, hop_ref),
                (cross_in, cross_ref),
                (deform_in, deform_ref),
                (test_in, tests.at[own_tests, :]),
            )
        )
    ]
    for load in loads:
        load.start()
    barrier = pltpu.get_barrier_semaphore()

    def others(act):
        for there_tile in range(T):

            def body(off, carry, there_tile=there_tile):
                act(there_tile, lax.rem(cut + off, S))
                return carry

            lax.fori_loop(jnp.where(tile == there_tile, 1, 0), S, body, 0)

    others(
        lambda t, c: pl.semaphore_signal(barrier, inc=1, device_id=(c, t), device_id_type=MESH)
    )

    slots[...] = jnp.zeros_like(slots)
    for load in loads[:3]:
        load.wait()
    for k in range(6):
        for i in range(NS):
            slots[k : k + 1, i * SC : (i + 1) * SC] = elastic_ref[k, i : i + 1, :]
    held = slots[...]
    turned = [held] + [pltpu.roll(held, SC * d, 1) for d in range(1, NS)]
    lane = lax.broadcasted_iota(jnp.int32, (8, X), 1)
    group = lane // SC
    own_ids = [ids_ref[tile * NS + i] for i in range(NS)]
    for t in range(T):
        placed = jnp.zeros((8, X), jnp.float32)
        for i in range(NS):
            for g in range(NS):
                wanted = jnp.where(group == g, t * NS + g, -1)
                placed = jnp.where(wanted == own_ids[i], turned[(g - i) % NS], placed)
        for w in range(W):
            row = (t * W + w) * msg
            for i in range(npr):
                send[row + i * B : row + (i + 1) * B, :] = probe_ref[
                    pl.ds(w * npr + i, B, stride=R), :
                ]
            send[row + chunk : row + msg, :] = placed
    for load in loads[3:]:
        load.wait()

    pl.semaphore_wait(barrier, N - 1)

    def message(target_tile, target_cut, near):
        source = (target_tile * W + lax.rem(target_cut, W)) * msg
        landing = (tile * S + cut) * msg
        skip = 0 if near else chunk
        return pltpu.make_async_remote_copy(
            src_ref=send.at[pl.ds(pl.multiple_of(source + skip, 8), msg - skip), :],
            dst_ref=got.at[pl.ds(pl.multiple_of(landing + skip, 8), msg - skip), :],
            send_sem=send_sem.at[0],
            recv_sem=got_sem.at[tile],
            device_id=(target_cut, target_tile),
            device_id_type=MESH,
        )

    def edge_copy(side):
        return pltpu.make_async_remote_copy(
            src_ref=edges.at[1],
            dst_ref=edges.at[2 - side],
            send_sem=edge_send.at[side],
            recv_sem=edge_sem.at[2 - side],
            device_id=(cut, tile + side - 1),
            device_id_type=MESH,
        )

    has_side = {0: tile > 0, 2: tile < T - 1}
    for side in (0, 2):
        pl.when(has_side[side])(lambda side=side: edge_copy(side).start())

    for there in range(T):
        near = jnp.abs(tile - there) <= 1
        low = jnp.where(tile == there, 1, 0)

        def pushes(near, there=there, low=low):
            def body(off, carry):
                message(there, lax.rem(cut + off, S), near).start()
                return carry

            lax.fori_loop(low, S, body, 0)

        pl.when(near)(lambda pushes=pushes: pushes(True))
        pl.when(jnp.logical_not(near))(lambda pushes=pushes: pushes(False))

    def awaited(ref, send, recv):
        return pltpu.make_async_remote_copy(
            src_ref=ref,
            dst_ref=ref,
            send_sem=send,
            recv_sem=recv,
            device_id=(cut, tile),
            device_id_type=MESH,
        )

    def settle(act):
        for there in range(T):
            gap = jnp.abs(tile - there)
            for wanted, rows in (
                (gap == 0, (S - 1) * msg),
                (gap == 1, S * msg),
                (gap > 1, S * (msg - chunk)),
            ):
                place = got.at[pl.ds(there * S * msg, rows), :]
                pl.when(wanted)(
                    lambda place=place, there=there: act(
                        awaited(place, send_sem.at[0], got_sem.at[there])
                    )
                )

    here = pl.multiple_of((tile * S + cut) * msg, 8)
    mine = pl.multiple_of((tile * W + lax.rem(cut, W)) * msg, 8)
    got[pl.ds(here, msg), :] = send[pl.ds(mine, msg), :]

    band = lax.broadcasted_iota(jnp.int32, (B, X), 0)
    hop = jnp.zeros((B, X), jnp.float32)
    for b in range(B):
        hop = jnp.where(band == b, hop_ref[b], hop)

    def fill_green(row):
        parts = line_green(edges[row], hop, S)
        for f in range(F):
            for d in range(D):
                green[row, f * D + d] = parts[f][d]
        return parts

    parts = fill_green(1)
    for p in range(NMOM):
        for j in range(HALF):
            wr = 2.0 * math.cos((p + 1) * ANGLES[j]) / PTS
            wi = 2.0 * math.sin((p + 1) * ANGLES[j]) / PTS
            for d in range(D):
                re, im = parts[2 * j][d], parts[2 * j + 1][d]
                final[(p * D + d) * F + 2 * j] = wr * re - wi * im
                final[(p * D + d) * F + 2 * j + 1] = -(wr * im + wi * re)
    def run(low, high, act):
        def body(off, carry):
            act(off)
            return carry

        lax.fori_loop(low, high, body, 0)

    def test_copy(off):
        other = lax.rem(cut + off, S)
        return pltpu.make_async_remote_copy(
            src_ref=tests.at[own_tests, :],
            dst_ref=tests.at[own_tests, :],
            send_sem=test_send.at[0],
            recv_sem=test_sem.at[0],
            device_id=(other, tile),
            device_id_type=MESH,
        )

    run(1, S, lambda off: test_copy(off).start())

    for side in (0, 2):

        @pl.when(has_side[side])
        def _(side=side):
            edge_copy(2 - side).wait_recv()
            fill_green(side)

    settle(lambda copy: copy.wait_recv())

    def solve_row(row):
        base = (tile + row - 1) * (S * msg)

        def body(b, carry):
            sums = []
            for i in range(npr):
                line = got[pl.ds(base + i * B + b, S, stride=msg), :]
                pairs = [line]
                for d in range(1, half):
                    pairs.append(pltpu.roll(line, d, 0) + pltpu.roll(line, S - d, 0))
                pairs.append(pltpu.roll(line, half, 0))
                sums.append(pairs)
            for f in range(F):
                totals = [None] * npr
                for d in range(D):
                    factor = green[row, f * D + d, pl.ds(b, 1), :]
                    for i in range(npr):
                        term = factor * sums[i][d]
                        totals[i] = term if totals[i] is None else totals[i] + term
                for i in range(npr):
                    first[row, b, f * npr + i] = totals[i]
            return carry

        lax.fori_loop(0, B, body, 0)

    solve_row(1)
    for side in (0, 2):
        pl.when(has_side[side])(lambda side=side: solve_row(side))

        @pl.when(jnp.logical_not(has_side[side]))
        def _(side=side):
            def clear(b, carry):
                first[side, b] = jnp.zeros_like(first[side, 0])
                return carry

            lax.fori_loop(0, B, clear, 0)

    strain = []
    for k in range(6):
        total = None
        for t in range(T):
            term = got[pl.ds(t * S * msg + chunk + k, S, stride=msg), :]
            total = term if total is None else total + term
        strain.append(total)
    for b in range(B):
        for c in range(b, B):
            total = None
            for k in range(6):
                term = (0.5 * (deform_ref[k, b, c] + deform_ref[k, c, b])) * strain[k]
                total = term if total is None else total + term
            mixer[b, c] = total
            if c != b:
                mixer[c, b] = total

    lanes = lax.broadcasted_iota(jnp.int32, (1, 1, X), 2)
    block = max(1, 8 * 8 // S)
    pieces = F * npr // block

    def couple(step, carry):
        b, piece = step // pieces, lax.rem(step, pieces)
        pick = pl.ds(piece * block, block)
        right = left = stay = None
        for c in range(B):
            u = first[1, c, pick]
            up, down = first[2, c, pick], first[0, c, pick]
            a = cross_ref[0, b, c] * u
            l = cross_ref[0, c, b] * u
            s = mixer[b, c][None] * u + cross_ref[1, b, c] * up + cross_ref[1, c, b] * down
            right = a if right is None else right + a
            left = l if left is None else left + l
            stay = s if stay is None else stay + s
        flat = (block * S, X)
        right = pltpu.roll(right.reshape(flat), X - 1, 1).reshape(block, S, X)
        left = pltpu.roll(left.reshape(flat), 1, 1).reshape(block, S, X)
        stay = stay + jnp.where(lanes < X - 1, right, 0.0) + jnp.where(lanes > 0, left, 0.0)
        second[b, pick] = stay
        return carry

    lax.fori_loop(0, B * pieces, couple, 0)

    def moments(b, carry):
        ys = [[second[b, f * npr + i] for f in range(F)] for i in range(npr)]
        for p in range(NMOM):
            totals = [None] * npr
            for j in range(HALF):
                wr = 2.0 * math.cos((p + 1) * ANGLES[j]) / PTS
                wi = 2.0 * math.sin((p + 1) * ANGLES[j]) / PTS
                for i in range(npr):
                    re, im = (first[1, b, (2 * j + comp) * npr + i] for comp in range(2))
                    term = wr * re - wi * im
                    totals[i] = term if totals[i] is None else totals[i] + term
            for d in range(D):
                zs = [None] * npr
                for f in range(F):
                    factor = final[(p * D + d) * F + f, pl.ds(b, 1), :]
                    for i in range(npr):
                        term = factor * ys[i][f]
                        zs[i] = term if zs[i] is None else zs[i] + term
                for i in range(npr):
                    if d == 0:
                        totals[i] = totals[i] + zs[i]
                    elif d == half:
                        totals[i] = totals[i] + pltpu.roll(zs[i], half, 0)
                    else:
                        turned_z = pltpu.roll(zs[i], d, 0) + pltpu.roll(zs[i], S - d, 0)
                        totals[i] = totals[i] + turned_z
            for i in range(npr):
                back[pl.ds((p * npr + i) * B + b, S, stride=ret), :] = totals[i]
        return carry

    lax.fori_loop(0, B, moments, 0)

    mates = (cut // W) * W
    rank = lax.rem(cut, W)

    landing = pl.multiple_of(rank * kept, 8)

    def home_copy(off):
        other = lax.rem(rank + off, W)
        source = pl.multiple_of((mates + other) * ret, 8)
        return pltpu.make_async_remote_copy(
            src_ref=back.at[pl.ds(source, kept), :],
            dst_ref=home.at[pl.ds(landing, kept), :],
            send_sem=back_send.at[0],
            recv_sem=home_sem.at[0],
            device_id=(mates + other, tile),
            device_id_type=MESH,
        )

    run(1, W, lambda off: home_copy(off).start())
    home[pl.ds(landing, kept), :] = back[
        pl.ds(pl.multiple_of(cut * ret, 8), kept), :
    ]

    all_tests = awaited(tests.at[pl.ds(0, (S - 1) * B * R), :], test_send.at[0], test_sem.at[0])
    all_tests.wait_recv()

    def halves(values):
        high = values.astype(jnp.bfloat16)
        return high, (values - high.astype(jnp.float32)).astype(jnp.bfloat16)

    def product(left, right):
        return lax.dot_general(
            left, right, (((1,), (1,)), ((), ())), preferred_element_type=jnp.float32
        )

    def by_slice(ref, rows):
        return halves(
            jnp.concatenate([ref[s * rows : (s + 1) * rows, :] for s in range(S)], axis=1)
        )

    high, low = by_slice(back, ret)
    test_high, test_low = by_slice(tests, B * R)
    acc = product(high, test_low) + product(low, test_high) + product(high, test_high)
    acc = acc.reshape(NMOM * npr, B, B * R)
    lane_band = lax.broadcasted_iota(jnp.int32, acc.shape, 2) // R
    same = lane_band == lax.broadcasted_iota(jnp.int32, acc.shape, 1)
    acc = jnp.sum(jnp.where(same, acc, 0.0), axis=1)
    total = acc
    for b in range(1, B):
        total = total + pltpu.roll(acc, b * R, 1)
    lane_row = lax.broadcasted_iota(jnp.int32, total.shape, 1) // R
    chosen = lane_row == lax.broadcasted_iota(jnp.int32, total.shape, 0)
    total = jnp.sum(jnp.where(chosen, total, 0.0), axis=0, keepdims=True)
    parts_all[me] = total * ((S * B * T * X) ** (-0.5))

    def part_copy(there_tile, there_cut):
        return pltpu.make_async_remote_copy(
            src_ref=parts_all.at[me],
            dst_ref=parts_all.at[me],
            send_sem=part_send.at[0],
            recv_sem=part_sem.at[0],
            device_id=(there_cut, there_tile),
            device_id_type=MESH,
        )

    others(lambda t, c: part_copy(t, c).start())

    all_home = awaited(home.at[pl.ds(0, (W - 1) * kept), :], back_send.at[0], home_sem.at[0])
    all_home.wait_recv()
    for w in range(W):
        for p in range(NFIELD):
            for i in range(npr):
                row = w * kept + (p * npr + i) * B
                field_ref[pl.ds(p * B * R + w * npr + i, B, stride=R), :] = home[row : row + B, :]

    settle(lambda copy: copy.wait_send())
    for side in (0, 2):
        pl.when(has_side[side])(lambda side=side: edge_copy(side).wait_send())
    all_tests.wait_send()
    all_home.wait_send()
    all_parts = awaited(parts_all.at[pl.ds(0, N - 1)], part_send.at[0], part_sem.at[0])
    all_parts.wait_recv()
    for w in range(W):
        total = parts_all[w * T]
        for t in range(1, T):
            total = total + parts_all[w * T + t]
        proj_ref[w : w + 1, :] = total
    all_parts.wait_send()


def on_device(
    S, T, probes, test_block, band_edge, slice_hop, cross_hop, deform, strain_elastic, strain_ids
):
    _, B, R, _, X = probes.shape
    NS, SC = strain_elastic.shape[1], strain_elastic.shape[3]
    dims = (S, T, B, R, X, NS, SC)
    W = min(S, R)
    npr = R // W
    D = S // 2 + 1
    F = 2 * HALF
    chunk = npr * B
    msg = chunk + 8
    ret = NMOM * chunk
    kept = NFIELD * chunk
    hbm = pl.BlockSpec(memory_space=pltpu.HBM)
    vmem = pl.BlockSpec(memory_space=pltpu.VMEM)
    f32 = jnp.float32
    dma = pltpu.SemaphoreType.DMA
    fields, proj = pl.pallas_call(
        functools.partial(kernel, dims),
        out_shape=(
            jax.ShapeDtypeStruct((NFIELD * B * R, X), f32),
            jax.ShapeDtypeStruct((W, B * R), f32),
        ),
        in_specs=[hbm] * 8,
        out_specs=(vmem, vmem),
        scratch_shapes=[
            pltpu.SMEM(strain_ids.shape, jnp.int32),
            pltpu.SMEM(slice_hop.shape, f32),
            pltpu.SMEM(cross_hop.shape, f32),
            pltpu.SMEM(deform.shape, f32),
            pltpu.VMEM((B * R, X), f32),
            pltpu.VMEM((6, NS, SC), f32),
            pltpu.VMEM((S * B * R, X), f32),
            pltpu.VMEM((8, X), f32),
            pltpu.VMEM((T * W * msg, X), f32),
            pltpu.VMEM((T * S * msg, X), f32),
            pltpu.VMEM((3, B, X), f32),
            pltpu.VMEM((3, F * D, B, X), f32),
            pltpu.VMEM((B, B, S, X), f32),
            pltpu.VMEM((3, B, F * npr, S, X), f32),
            pltpu.VMEM((B, F * npr, S, X), f32),
            pltpu.VMEM((S * ret, X), f32),
            pltpu.VMEM((W * kept, X), f32),
            pltpu.VMEM((NMOM * D * F, B, X), f32),
            pltpu.VMEM((S * T, 1, B * R), f32),
            dma((8,)),
            dma((1,)),
            dma((T,)),
            dma((3,)),
            dma((3,)),
            dma((1,)),
            dma((1,)),
            dma((1,)),
            dma((1,)),
            dma((1,)),
            dma((1,)),
        ],
        compiler_params=pltpu.CompilerParams(
            collective_id=0, has_side_effects=True, vmem_limit_bytes=63 * 1024 * 1024
        ),
    )(
        strain_ids,
        slice_hop,
        cross_hop,
        deform,
        probes.reshape(B * R, X),
        test_block.reshape(B * R, X),
        band_edge.reshape(B, X),
        jnp.transpose(strain_elastic[0], (1, 0, 2)),
    )
    fields = fields.reshape(NFIELD, 1, 1, B, R, 1, X)
    fields = jnp.concatenate([fields, jnp.zeros_like(fields)], axis=1)
    proj = proj[:, : NMOM * npr * R].reshape(W, NMOM, npr, R)
    proj = jnp.transpose(proj, (1, 3, 0, 2)).reshape(NMOM, 1, R, R)
    return fields, jnp.concatenate([proj, jnp.zeros_like(proj)], axis=1)


def solution(mesh):
    placed = (
        P("cuts", None, None, "tile", None),
        P("cuts", None, None, "tile", None),
        P(None, "tile", None),
        P(),
        P(),
        P(),
        P("cuts", "tile", None, None),
        P(),
    )
    return jax.shard_map(
        functools.partial(on_device, mesh.shape["cuts"], mesh.shape["tile"]),
        mesh=mesh,
        in_specs=placed,
        out_specs=(P(None, None, "cuts", None, None, "tile", None), P()),
        check_vma=False,
    )
```
